256 devices in a mesh: prow: 8 (over z), pcol: 32 (over y, x, core).
Axes of the slice: x: 4, y: 4, z: 8, core: 2. Of those that a mesh axis runs over, the one named last changes fastest.
Arguments:
- matrix: bfloat16 [24576, 32768], P('prow', 'pcol'), may hold values from -6 to 6
- pivots: int32 [2, 128], replicated, may hold values from 0 to 24575, as said below
- col_blocks: int32 [256], replicated, may hold values from 0 to 255, each once
- lower_inv: float32 [2, 128, 128], replicated, as said below
- upper_inv: float32 [2, 128, 128], replicated, as said below
Outputs:
- updated: bfloat16 [24576, 32768], P('prow', 'pcol')
The draws below stay inside these ranges and needn't reach their ends.
Inputs may be any that keep to these rules, and one draw needn't show every extreme that they name: pivots[k, i] is at least k * 128 + i. `col_blocks`: each column block is stored in exactly one slot. lower_inv[k] is unit lower triangular. upper_inv[k] is upper triangular with a positive diagonal.
All inputs are finite; a program needn't handle non-finite values.
Results may differ from the reference program's by a relative error of at most 0.0077.
Values may be sent and summed in bfloat16 or wider, within the bound.
No kernel may reach another device: no remote copies, remote signals or barrier semaphores. Data moves between devices by JAX's collectives and lax.ppermute only.
A program may use at most 64 MiB of HBM per device.

```python
import jax
import jax.numpy as jnp
from jax import lax

NB = 128
PANELS = 2
ROWS = 24576
COLS = 32768
NBC = 256
N_PROW = 8


def triangle_masks():
    indices = jnp.arange(NB, dtype=jnp.int32)
    return (indices[:, None] > indices[None, :], indices[:, None] == indices[None, :])


def draw_pivots(key, part):
    key = jax.random.fold_in(key, 5)
    first_key, second_key = jax.random.split(key)
    lowest = jnp.arange(PANELS, dtype=jnp.int32)[:, None] * NB + jnp.arange(NB, dtype=jnp.int32)[None, :]
    drawn_rows = jax.random.randint(first_key, (PANELS, NB), lowest, ROWS, dtype=jnp.int32)
    chosen = jax.random.randint(second_key, (PANELS, 1), 0, NB, dtype=jnp.int32)
    return jnp.where(jnp.arange(NB, dtype=jnp.int32)[None, :] == chosen, ROWS - 1, drawn_rows).astype(jnp.int32)


def draw_lower_inv(key, part):
    key = jax.random.fold_in(key, 11)
    below, diagonal = triangle_masks()
    values = jax.random.uniform(key, (PANELS, NB, NB), jnp.float32, -0.2, 0.2)
    return jnp.where(below, values, jnp.where(diagonal, 1.0, 0.0)).astype(jnp.float32)


def draw_upper_inv(key, part):
    key = jax.random.fold_in(key, 23)
    first_key, second_key = jax.random.split(key)
    below, diagonal = triangle_masks()
    values = jax.random.uniform(first_key, (PANELS, NB, NB), jnp.float32, -0.008, 0.008)
    scales = 0.05 * jnp.exp(jax.random.uniform(second_key, (PANELS, NB, NB), jnp.float32, -0.6931, 0.6931))
    above = jnp.logical_not(jnp.logical_or(below, diagonal))
    return jnp.where(above, values, jnp.where(diagonal, scales, 0.0)).astype(jnp.float32)


def shard_levels(own_key, dims, cuts, low, largest):
    factor_of = 1.0
    for axis_at, shards_of in cuts:
        steps = jax.random.uniform(jax.random.fold_in(jax.random.fold_in(own_key, 6), axis_at), (shards_of,), jnp.float32, low / len(cuts), largest / len(cuts))
        factor_of = factor_of * jnp.repeat(jnp.exp(steps), dims[axis_at] // shards_of).reshape((-1,) + (1,) * (len(dims) - 1 - axis_at))
    return factor_of


def centred(own_key, shape, spread, limit, pieces=(), kind=jnp.bfloat16):
    values = spread * jax.random.normal(own_key, shape, jnp.float32)
    if pieces:
        values = values * shard_levels(own_key, shape, pieces, -0.22, 0.18)
    return jnp.clip(values, -limit, limit).astype(kind)


def setup_inputs(seed: int = 0) -> dict:
    streams_of = jax.random.split(jax.random.key(seed), 6)
    matrix = centred(streams_of[0], (ROWS, COLS), 1.0, 6.0, ((0, 8), (1, 32)))
    pivots = draw_pivots(jax.random.fold_in(streams_of[5], 71), 0)
    col_blocks = jax.random.permutation(streams_of[2], NBC).astype(jnp.int32)
    lower_inv = draw_lower_inv(jax.random.fold_in(streams_of[5], 71), 0)
    upper_inv = draw_upper_inv(jax.random.fold_in(streams_of[5], 71), 0)
    return {"matrix": matrix, "pivots": pivots, "col_blocks": col_blocks, "lower_inv": lower_inv, "upper_inv": upper_inv}


def compose(pivot_row, first_row, total_rows):
    def exchange_pair(column, ordering):
        top_pos = first_row + column
        far_pos = pivot_row[column]
        top_value = ordering[top_pos]
        far_value = ordering[far_pos]
        return ordering.at[top_pos].set(far_value).at[far_pos].set(top_value)

    return lax.fori_loop(0, pivot_row.shape[0], exchange_pair, jnp.arange(total_rows, dtype=jnp.int32))


def reference(matrix, pivots, col_blocks, lower_inv, upper_inv):
    total_rows, total_cols = matrix.shape
    block_size = lower_inv.shape[-1]
    rows_here = total_rows // N_PROW
    storage = jnp.arange(total_rows, dtype=jnp.int32)
    within = storage % rows_here
    global_rows = ((within // block_size) * N_PROW + storage // rows_here) * block_size + within % block_size
    storage_of = jnp.zeros((total_rows,), jnp.int32).at[global_rows].set(storage)
    global_cols = jnp.repeat(col_blocks, block_size) * block_size + jnp.arange(total_cols, dtype=jnp.int32) % block_size
    slot_ids = jnp.arange(col_blocks.shape[0], dtype=jnp.int32)
    current = matrix
    for step_index in range(PANELS):
        first_row = step_index * block_size
        ordering = compose(pivots[step_index], first_row, total_rows)
        top_global = first_row + jnp.arange(block_size, dtype=jnp.int32)
        targets = jnp.concatenate([top_global, pivots[step_index]])
        current = current.at[storage_of[targets]].set(current[storage_of[ordering[targets]]])
        position = jnp.sum(jnp.where(col_blocks == step_index, slot_ids, 0)).astype(jnp.int32)
        panel_cols = lax.dynamic_slice_in_dim(current, position * block_size, block_size, 1)
        trail_rows = (global_rows >= first_row + block_size)[:, None]
        factored = jnp.dot(panel_cols.astype(jnp.float32), upper_inv[step_index], precision=lax.Precision.HIGHEST).astype(jnp.bfloat16)
        lowered = jnp.where(trail_rows, factored, jnp.zeros_like(factored))
        current = lax.dynamic_update_slice_in_dim(current, jnp.where(trail_rows, factored, panel_cols), position * block_size, 1)
        top_rows = current[storage_of[top_global]]
        trail_cols = (global_cols >= first_row + block_size)[None, :]
        upper_part = jnp.dot(lower_inv[step_index], top_rows.astype(jnp.float32), precision=lax.Precision.HIGHEST).astype(jnp.bfloat16)
        upper_zero = jnp.where(trail_cols, upper_part, jnp.zeros_like(upper_part)).astype(jnp.float32)
        current = current.at[storage_of[top_global]].set(jnp.where(trail_cols, upper_part, top_rows))

        def lower_rows(blocks_pair):
            rows_block, factors = blocks_pair
            product = jnp.dot(factors.astype(jnp.float32), upper_zero, precision=lax.Precision.HIGHEST)
            return (rows_block.astype(jnp.float32) - product).astype(jnp.bfloat16)

        stacked = current.reshape(total_rows // block_size, block_size, total_cols)
        factor_rows = lowered.reshape(total_rows // block_size, block_size, block_size)
        current = lax.map(lower_rows, (stacked, factor_rows)).reshape(total_rows, total_cols)
    return current
```

```python
import jax
import jax.numpy as jnp
from jax import lax
from jax.experimental import pallas as pl
from jax.experimental.pallas import tpu as pltpu
from jax.sharding import PartitionSpec as P

NB = 128
TOP = 2 * NB
PY, PX, CORES = 4, 4, 2
VMEM_BYTES = 50 * 1024 * 1024

BF = jnp.bfloat16
F32 = jnp.float32


def split3(x):
    high = x.astype(BF)
    rest = x - high.astype(F32)
    mid = rest.astype(BF)
    low = (rest - mid.astype(F32)).astype(BF)
    return high, mid, low


def dot(a, b):
    return jnp.dot(a, b, preferred_element_type=F32)


def dot_right(x, w):
    high, mid, low = split3(w)
    return dot(x, low) + dot(x, mid) + dot(x, high)


def dot_left(w, x):
    high, mid, low = split3(w)
    return dot(low, x) + dot(mid, x) + dot(high, x)


def local_row(rows, prow, prow_count):
    here = (rows // NB) % prow_count == prow
    return jnp.where(here & (rows >= 0), rows // (NB * prow_count) * NB + rows % NB, -1)


def fetch_kernel(prow_count, where_ref, piv_hbm, cols_hbm, a_ref, index_ref, rows_ref, own_ref, send_ref, order, piv_ref, cols_ref, slab, picked, sems, panel_sems, top_sems):
    prow, core = where_ref[0], where_ref[2]
    slots = a_ref.shape[1] // NB
    chunk_top = 3 * NB // PY
    block_rows = a_ref.shape[0] // PY
    firsts = (
        pltpu.make_async_copy(cols_hbm, cols_ref, top_sems.at[0]),
        pltpu.make_async_copy(piv_hbm, piv_ref, top_sems.at[1]),
        pltpu.make_async_copy(a_ref.at[pl.ds(0, NB), :], rows_ref.at[pl.ds(TOP, NB), :], top_sems.at[2]),
    )
    for copy in firsts:
        copy.start()
    firsts[0].wait()

    def place(t, carry):
        index_ref[1, cols_ref[t]] = t
        return carry

    lax.fori_loop(0, cols_ref.shape[0], place, 0, unroll=16)
    copies = []
    for n, (out, panel) in enumerate(((own_ref, core), (send_ref, 1 - core))):
        start = pl.multiple_of(index_ref[1, panel] % slots * NB, NB)
        for j in range(PY):
            copies.append(
                pltpu.make_async_copy(
                    a_ref.at[pl.ds(j * block_rows, block_rows), pl.ds(start, NB)],
                    out.at[j, pl.ds(chunk_top, block_rows), :],
                    panel_sems.at[n, j],
                )
            )
    for copy in copies:
        copy.start()

    def init(t, carry):
        order[t] = t
        index_ref[0, t] = -1
        return carry

    lax.fori_loop(0, TOP, init, 0, unroll=16)
    firsts[1].wait()
    for k in range(2):

        def untouched(i, carry):
            far = piv_ref[k, i]
            order[far] = far
            return carry

        lax.fori_loop(0, NB, untouched, 0, unroll=16)
    for k in range(2):

        def exchange(i, carry):
            far = piv_ref[k, i]
            near_value = order[k * NB + i]
            far_value = order[far]
            order[k * NB + i] = far_value
            order[far] = near_value
            return carry

        lax.fori_loop(0, NB, exchange, 0, unroll=16)

    def held(g):
        row = order[g]
        return (row >> 7) & (prow_count - 1) == prow, (row >> 10) * NB + (row & (NB - 1))

    def slab_copy(g, line):
        first = pl.multiple_of(line >> 4 << 4, 16)
        return pltpu.make_async_copy(a_ref.at[pl.ds(first, 16), :], slab.at[g], sems.at[g])

    def begin(g, carry):
        here, line = held(g)

        @pl.when(here)
        def _():
            slab_copy(g, line).start()

        return carry

    lax.fori_loop(0, TOP, begin, 0, unroll=8)
    picked[...] = jnp.zeros_like(picked)
    for k in range(2):

        def emit(i, carry):
            far = piv_ref[k, i]
            below = far >= TOP
            index_ref[0, jnp.where(below, order[far], TOP)] = jnp.where(below, far, -1)
            return carry

        lax.fori_loop(0, NB, emit, 0, unroll=16)
    line16 = lax.broadcasted_iota(jnp.int32, (16, a_ref.shape[1]), 0)

    def take(g, carry):
        here, line = held(g)

        @pl.when(here)
        def _():
            slab_copy(g, line).wait()
            chosen = jnp.where(line16 == (line & 15), slab[g].astype(F32), 0.0)
            picked[pl.ds(g, 1), :] = jnp.sum(chosen, axis=0, keepdims=True)

        return carry

    lax.fori_loop(0, TOP, take, 0, unroll=2)
    rows_ref[0:TOP, :] = picked[...].astype(BF)
    firsts[2].wait()
    old = rows_ref[TOP:TOP + NB, :]
    zero = jnp.zeros_like(old)
    rows_ref[TOP:TOP + NB, :] = jnp.where(prow == 0, old, zero)
    rows_ref[TOP + NB:, :] = jnp.where(prow == 1, old, zero)
    for copy in copies:
        copy.wait()
    for out, panel in ((own_ref, core), (send_ref, 1 - core)):
        start = pl.multiple_of(index_ref[1, panel] % slots * NB, NB)
        near = rows_ref[pl.ds(pl.multiple_of((1 - panel) * NB, NB), NB), pl.ds(start, NB)]
        small = jnp.concatenate([near, rows_ref[TOP:, pl.ds(start, NB)]], axis=0)
        for j in range(PY):
            out[j, 0:chunk_top, :] = small[j * chunk_top:(j + 1) * chunk_top]


def fetch(where, pivots, col_blocks, matrix, prow_count):
    rows_here, cols_here = matrix.shape
    chunk = (rows_here + 3 * NB) // PY
    smem = pl.BlockSpec(memory_space=pltpu.SMEM)
    vmem = pl.BlockSpec(memory_space=pltpu.VMEM)
    hbm = pl.BlockSpec(memory_space=pl.ANY)
    return pl.pallas_call(
        lambda *refs: fetch_kernel(prow_count, *refs),
        out_shape=(
            jax.ShapeDtypeStruct((2, 2 * TOP), jnp.int32),
            jax.ShapeDtypeStruct((2 * TOP, cols_here), BF),
            jax.ShapeDtypeStruct((PY, chunk, NB), BF),
            jax.ShapeDtypeStruct((PY, chunk, NB), BF),
        ),
        in_specs=[smem, hbm, hbm, hbm],
        out_specs=(smem, vmem, vmem, vmem),
        scratch_shapes=[
            pltpu.SMEM((rows_here * prow_count,), jnp.int32),
            pltpu.SMEM(pivots.shape, jnp.int32),
            pltpu.SMEM(col_blocks.shape, jnp.int32),
            pltpu.VMEM((TOP, 16, cols_here), BF),
            pltpu.VMEM((TOP, cols_here), F32),
            pltpu.SemaphoreType.DMA((TOP,)),
            pltpu.SemaphoreType.DMA((2, PY)),
            pltpu.SemaphoreType.DMA((3,)),
        ],
        compiler_params=pltpu.CompilerParams(vmem_limit_bytes=VMEM_BYTES),
        name="fetch",
    )(where, pivots, col_blocks, matrix)


def factor_kernel(prow_count, where_ref, index_vec, mine_ref, other_ref, lower_ref, upper_ref, out_ref, low_ref):
    prow, core = where_ref[0], where_ref[2]
    chunk = mine_ref.shape[1]
    chunk_top = 3 * NB // PY
    block_rows = chunk - chunk_top

    def panel(k, j, part):
        mine, other = mine_ref[j, part, :], other_ref[j, part, :]
        return jnp.where(core == k, mine, other)

    small = [jnp.concatenate([panel(k, j, slice(0, chunk_top)) for j in range(PY)], axis=0) for k in range(2)]
    near_mid, near_top = small[0][0:NB], small[1][0:NB]
    far = [small[0][NB:], small[1][NB:]]
    top_mid = dot_left(lower_ref[0], near_top).astype(BF)
    low_ref[...] = dot_right(near_mid, upper_ref[0]).astype(BF)
    dest = local_row(index_vec[0:1, 0:TOP], prow, prow_count)
    for j in range(PY):
        line = lax.broadcasted_iota(jnp.int32, (block_rows, TOP), 0) + j * block_rows
        hot = jnp.where(line == dest, 1.0, 0.0)
        kept = jnp.sum(hot, axis=1, keepdims=True) == 0.0
        hot = hot.astype(BF)
        raw = [
            jnp.where(kept, panel(k, j, slice(chunk_top, chunk)).astype(F32), dot(hot, far[k])) for k in range(2)
        ]
        first = dot_right(raw[0].astype(BF), upper_ref[0]).astype(BF)
        if j == 0:
            above = (lax.broadcasted_iota(jnp.int32, (block_rows, NB), 0) < NB) & (prow == 0)
            first = jnp.where(above, jnp.zeros_like(first), first)
        middle = (raw[1] - dot(first, top_mid)).astype(BF)
        second = dot_right(middle, upper_ref[1]).astype(BF)
        if j == 0:
            above = (lax.broadcasted_iota(jnp.int32, (block_rows, NB), 0) < NB) & (prow < 2)
            second = jnp.where(above, jnp.zeros_like(second), second)
        out_ref[j * block_rows:(j + 1) * block_rows, 0:NB] = first
        out_ref[j * block_rows:(j + 1) * block_rows, NB:] = second


def factor(where, index, mine, other, lower_inv, upper_inv, prow_count):
    rows_here = PY * (mine.shape[1] - 3 * NB // PY)
    smem = pl.BlockSpec(memory_space=pltpu.SMEM)
    vmem = pl.BlockSpec(memory_space=pltpu.VMEM)
    return pl.pallas_call(
        lambda *refs: factor_kernel(prow_count, *refs),
        out_shape=(jax.ShapeDtypeStruct((rows_here, TOP), BF), jax.ShapeDtypeStruct((NB, NB), BF)),
        in_specs=[smem] + [vmem] * 5,
        out_specs=(vmem, vmem),
        compiler_params=pltpu.CompilerParams(vmem_limit_bytes=VMEM_BYTES),
        name="factor",
    )(where, index, mine, other, lower_inv, upper_inv)


def update_kernel(prow_count, where_ref, index_ref, cols_ref, index_vec, rows_ref, low_ref, lower_ref, a_ref, l_ref, out_ref, right):
    step = pl.program_id(0)
    prow, pcol = where_ref[0], where_ref[1]
    block_rows, cols_here = a_ref.shape
    slots = cols_here // NB
    lanes = lambda s: slice(s * NB, (s + 1) * NB)

    @pl.when(step == 0)
    def _():
        top = dot_left(lower_ref[0], rows_ref[0:NB, :]).astype(BF)
        for s in range(slots):
            block = cols_ref[pcol * slots + s]
            right[0:NB, lanes(s)] = jnp.where(block >= 1, -top[:, lanes(s)], jnp.zeros((NB, NB), BF))
        mid = (rows_ref[NB:TOP, :].astype(F32) + dot(low_ref[...], right[0:NB, :])).astype(BF)
        low = dot_left(lower_ref[1], mid).astype(BF)
        for s in range(slots):
            block = cols_ref[pcol * slots + s]
            right[NB:TOP, lanes(s)] = jnp.where(block >= 2, -low[:, lanes(s)], jnp.zeros((NB, NB), BF))
        right[TOP:, :] = rows_ref[TOP:, :]

    line = lax.broadcasted_iota(jnp.int32, (block_rows, TOP), 0) + step * block_rows
    hot = jnp.where(line == local_row(index_vec[0:1, 0:TOP], prow, prow_count), 1.0, 0.0)
    kept = jnp.sum(hot, axis=1, keepdims=True) == 0.0
    left = jnp.concatenate([l_ref[...], hot.astype(BF)], axis=1)
    old = a_ref[...].astype(F32)
    out_ref[...] = (jnp.where(kept, old, 0.0) + dot(left, right[...])).astype(BF)

    for k in range(2):
        slot = index_ref[1, k]

        @pl.when(slot // slots == pcol)
        def _():
            start = pl.multiple_of(slot % slots * NB, NB)
            out_ref[:, pl.ds(start, NB)] = l_ref[:, k * NB:(k + 1) * NB]

    @pl.when((step == 0) & (prow == 0))
    def _():
        for s in range(slots):
            block = cols_ref[pcol * slots + s]
            out_ref[0:NB, lanes(s)] = jnp.where(block >= 1, -right[0:NB, lanes(s)], rows_ref[0:NB, lanes(s)])

    @pl.when((step == 0) & (prow == 1))
    def _():
        mid = (rows_ref[NB:TOP, :].astype(F32) + dot(low_ref[...], right[0:NB, :])).astype(BF)
        for s in range(slots):
            block = cols_ref[pcol * slots + s]
            changed = jnp.where(block == 1, mid[:, lanes(s)], -right[NB:TOP, lanes(s)])
            out_ref[0:NB, lanes(s)] = jnp.where(block == 0, low_ref[...], changed)


def update(where, index, col_blocks, rows, low, lower_inv, matrix, left, prow_count):
    rows_here, cols_here = matrix.shape
    steps = 6
    block_rows = rows_here // steps
    smem = pl.BlockSpec(memory_space=pltpu.SMEM)
    whole = lambda x: pl.BlockSpec(x.shape, lambda i: (0,) * x.ndim)
    return pl.pallas_call(
        lambda *refs: update_kernel(prow_count, *refs),
        grid=(steps,),
        out_shape=jax.ShapeDtypeStruct(matrix.shape, BF),
        in_specs=[
            smem,
            smem,
            smem,
            whole(index),
            whole(rows),
            whole(low),
            whole(lower_inv),
            pl.BlockSpec((block_rows, cols_here), lambda i: (i, 0)),
            pl.BlockSpec((block_rows, TOP), lambda i: (i, 0)),
        ],
        out_specs=pl.BlockSpec((block_rows, cols_here), lambda i: (i, 0)),
        scratch_shapes=[pltpu.VMEM((2 * TOP, cols_here), BF)],
        compiler_params=pltpu.CompilerParams(vmem_limit_bytes=VMEM_BYTES),
        name="update",
    )(where, index, col_blocks, index, rows, low, lower_inv, matrix, left)


CORE_SWAP = [(i, i ^ 1) for i in range(PY * PX * CORES)]
Y_GROUPS = [[(y * PX + x) * CORES + c for y in range(PY)] for x in range(PX) for c in range(CORES)]
X_GROUPS = [[(y * PX + x) * CORES + c for x in range(PX)] for y in range(PY) for c in range(CORES)]


def spread(x, axis, groups, count):
    x = jnp.broadcast_to(x[None], (count,) + x.shape)
    return lax.all_to_all(x, axis, 0, 0, axis_index_groups=groups)


def local(matrix, pivots, col_blocks, lower_inv, upper_inv):
    prow_count = lax.axis_size("prow")
    prow = lax.axis_index("prow")
    pcol = lax.axis_index("pcol")
    core = pcol % CORES
    where = jnp.stack([prow, pcol, core]).astype(jnp.int32)
    slots = matrix.shape[1] // NB

    index, rows, own, send = fetch(where, pivots, col_blocks, matrix, prow_count)
    rows = lax.psum(rows, "prow")

    def broadcast(own, send, index):
        owner = lax.dynamic_index_in_dim(index[1, :2], core, 0, keepdims=False) // slots
        received = lax.ppermute(send, "pcol", CORE_SWAP)
        panel = jnp.where(owner % CORES == core, own, received)
        panel = lax.all_to_all(panel, "pcol", 0, 0, axis_index_groups=Y_GROUPS)
        panel = lax.dynamic_index_in_dim(panel, owner // (CORES * PX), 0, keepdims=False)
        chunk_top = 3 * NB // PY
        small = jnp.sum(spread(panel[:chunk_top], "prow", None, prow_count), axis=0, dtype=BF)
        panel = jnp.concatenate([small, panel[chunk_top:]], axis=0)
        panel = spread(panel, "pcol", X_GROUPS, PX)
        panel = lax.dynamic_index_in_dim(panel, owner // CORES % PX, 0, keepdims=False)
        mine = spread(panel, "pcol", Y_GROUPS, PY)
        return mine, lax.ppermute(mine, "pcol", CORE_SWAP)

    mine, other = lax.cond(pivots[0, 0] >= 0, broadcast, lambda own, send, index: (own, send), own, send, index)
    left, low = factor(where, index, mine, other, lower_inv, upper_inv, prow_count)
    return update(where, index, col_blocks, rows, low, lower_inv, matrix, left, prow_count)


def solution(mesh):
    in_specs = (P("prow", "pcol"), P(), P(), P(), P())
    out_specs = P("prow", "pcol")
    return jax.shard_map(local, mesh=mesh, in_specs=in_specs, out_specs=out_specs, check_vma=False)
```

```python
import jax
import jax.numpy as jnp
from jax import lax
from jax.experimental import pallas as pl
from jax.experimental.pallas import tpu as pltpu
from jax.sharding import PartitionSpec as P

NB = 128
TOP = 2 * NB
PY, PX, CORES = 4, 4, 2
CHUNKS = PY
SMALL = 3 * NB
STEPS = 6
PLAN = 'U1 D1|U2 D2 U3 D3|U4 G1|G2|G3|G4'
VMEM_BYTES = 50 * 1024 * 1024

BF = jnp.bfloat16
F32 = jnp.float32


def split3(x):
    high = x.astype(BF)
    rest = x - high.astype(F32)
    mid = rest.astype(BF)
    low = (rest - mid.astype(F32)).astype(BF)
    return high, mid, low


def dot(a, b):
    return jnp.dot(a, b, preferred_element_type=F32)


def dot_right(x, w):
    high, mid, low = split3(w)
    return dot(x, low) + dot(x, mid) + dot(x, high)


def dot_left(w, x):
    high, mid, low = split3(w)
    return dot(low, x) + dot(mid, x) + dot(high, x)


def local_row(rows, prow, prow_count):
    here = (rows // NB) % prow_count == prow
    return jnp.where(here & (rows >= 0), rows // (NB * prow_count) * NB + rows % NB, -1)


def fetch_kernel(where_ref, piv_ref, meta_ref, a_ref, index_ref, parts_ref, own_ref, send_ref, order, held, slab, picked, old, sems, panel_sems, top_sem):
    prow, core = where_ref[0], where_ref[2]
    prow_count = parts_ref.shape[0]
    slots = a_ref.shape[1] // NB
    chunk_top = SMALL // CHUNKS
    block_rows = a_ref.shape[0] // CHUNKS
    top_part, old_part = TOP // prow_count, NB // prow_count
    old_copy = pltpu.make_async_copy(a_ref.at[pl.ds(0, NB), :], old, top_sem)
    old_copy.start()
    places = [
        jnp.sum(jnp.where(meta_ref[2:4, :] == k, meta_ref[4:6, :], 0).astype(F32)).astype(jnp.int32) for k in range(2)
    ]
    panels = []
    for n, (out, panel) in enumerate(((own_ref, core), (send_ref, 1 - core))):
        place = jnp.where(panel == 0, places[0], places[1])
        start = pl.multiple_of(place % slots * NB, NB)
        copies = [
            pltpu.make_async_copy(
                a_ref.at[pl.ds(j * block_rows, block_rows), pl.ds(start, NB)],
                out.at[j, pl.ds(chunk_top, block_rows), :],
                panel_sems.at[n, j],
            )
            for j in range(CHUNKS)
        ]
        panels.append((out, panel, start, place // slots % CORES == core, copies))

        @pl.when(panels[n][3])
        def _():
            for copy in copies:
                copy.start()

    for k in range(2):
        index_ref[TOP + k] = places[k]

    def init(t, carry):
        order[t] = t
        index_ref[t] = -1
        return carry

    lax.fori_loop(0, TOP, init, 0, unroll=TOP)

    def untouched(t, carry):
        far = piv_ref[t]
        order[far] = far
        return carry

    lax.fori_loop(0, TOP, untouched, 0, unroll=TOP)

    def exchange(t, carry):
        far = piv_ref[t]
        near_value = order[t]
        far_value = order[far]
        order[t] = far_value
        order[far] = near_value
        return carry

    lax.fori_loop(0, TOP, exchange, 0, unroll=TOP)

    def collect(g, count):
        held[count] = g
        return count + ((order[g] >> 7) & (prow_count - 1) == prow).astype(jnp.int32)

    count = lax.fori_loop(0, TOP, collect, 0, unroll=TOP)

    def line_of(n):
        row = order[held[n]]
        return (row >> 10) * NB + (row & (NB - 1))

    def slab_copy(n, line):
        first = pl.multiple_of(line >> 4 << 4, 16)
        return pltpu.make_async_copy(a_ref.at[pl.ds(first, 16), :], slab.at[n], sems.at[n])

    def begin(n, carry):
        slab_copy(n, line_of(n)).start()
        return carry

    lax.fori_loop(0, count, begin, 0)
    picked[...] = jnp.zeros_like(picked)

    def emit(t, carry):
        far = piv_ref[t]
        index_ref[jnp.where(far >= TOP, order[far], TOP + NB)] = far
        return carry

    lax.fori_loop(0, TOP, emit, 0, unroll=TOP)
    line16 = lax.broadcasted_iota(jnp.int32, (16, a_ref.shape[1]), 0)

    def take(n, carry):
        line = line_of(n)
        slab_copy(n, line).wait()
        chosen = jnp.where(line16 == (line & 15), slab[n].astype(F32), 0.0)
        picked[pl.ds(held[n], 1), :] = jnp.sum(chosen, axis=0, keepdims=True)
        return carry

    lax.fori_loop(0, count, take, 0)
    old_copy.wait()
    for q in range(prow_count):
        parts_ref[q, 0:top_part, :] = picked[q * top_part:(q + 1) * top_part, :].astype(BF)
        for k in range(2):
            first = top_part + k * old_part
            mine = old[q * old_part:(q + 1) * old_part, :]
            parts_ref[q, first:first + old_part, :] = jnp.where(prow == k, mine, jnp.zeros_like(mine))
    for out, panel, start, valid, copies in panels:

        @pl.when(valid)
        def _():
            near = picked[pl.ds(pl.multiple_of((1 - panel) * NB, NB), NB), pl.ds(start, NB)].astype(BF)
            far = old[:, pl.ds(start, NB)]
            zero = jnp.zeros_like(far)
            small = jnp.concatenate([near, jnp.where(prow == 0, far, zero), jnp.where(prow == 1, far, zero)], axis=0)
            for copy in copies:
                copy.wait()
            for j in range(CHUNKS):
                out[j, 0:chunk_top, :] = small[j * chunk_top:(j + 1) * chunk_top]

        @pl.when(jnp.logical_not(valid))
        def _():
            out[...] = jnp.zeros_like(out)


def fetch(where, meta, matrix, prow_count):
    rows_here, cols_here = matrix.shape
    chunk = (rows_here + SMALL) // CHUNKS
    part = 2 * TOP // prow_count
    smem = pl.BlockSpec(memory_space=pltpu.SMEM)
    vmem = pl.BlockSpec(memory_space=pltpu.VMEM)
    hbm = pl.BlockSpec(memory_space=pltpu.HBM)
    return pl.pallas_call(
        fetch_kernel,
        out_shape=(
            jax.ShapeDtypeStruct((2 * TOP,), jnp.int32),
            jax.ShapeDtypeStruct((prow_count, part, cols_here), BF),
            jax.ShapeDtypeStruct((CHUNKS, chunk, NB), BF),
            jax.ShapeDtypeStruct((CHUNKS, chunk, NB), BF),
        ),
        in_specs=[smem, smem, vmem, hbm],
        out_specs=(smem, vmem, vmem, vmem),
        scratch_shapes=[
            pltpu.SMEM((rows_here * prow_count,), jnp.int32),
            pltpu.SMEM((TOP + 1,), jnp.int32),
            pltpu.VMEM((TOP, 16, cols_here), BF),
            pltpu.VMEM((TOP, cols_here), F32),
            pltpu.VMEM((NB, cols_here), BF),
            pltpu.SemaphoreType.DMA((TOP,)),
            pltpu.SemaphoreType.DMA((2, CHUNKS)),
            pltpu.SemaphoreType.DMA(()),
        ],
        compiler_params=pltpu.CompilerParams(vmem_limit_bytes=VMEM_BYTES),
        name="fetch",
    )(where, meta, meta.reshape(-1, NB), matrix)


def factor_kernel(prow_count, where_ref, index_vec, mine_ref, other_ref, lower_ref, upper_ref, out_ref, low_ref):
    prow, core = where_ref[0], where_ref[2]
    chunk = mine_ref.shape[1]
    chunk_top = SMALL // CHUNKS
    block_rows = chunk - chunk_top

    def panel(k, j, part):
        mine, other = mine_ref[j, part, :], other_ref[j, part, :]
        return jnp.where(core == k, mine, other)

    small = [jnp.concatenate([panel(k, j, slice(0, chunk_top)) for j in range(CHUNKS)], axis=0) for k in range(2)]
    near_mid, near_top = small[0][0:NB], small[1][0:NB]
    far = [small[0][NB:NB + TOP], small[1][NB:NB + TOP]]
    top_mid = dot_left(lower_ref[0], near_top).astype(BF)
    low_ref[...] = dot_right(near_mid, upper_ref[0]).astype(BF)
    dest = local_row(jnp.concatenate([index_vec[0:1, :], index_vec[1:2, :]], axis=1), prow, prow_count)
    for j in range(CHUNKS):
        line = lax.broadcasted_iota(jnp.int32, (block_rows, TOP), 0) + j * block_rows
        hot = jnp.where(line == dest, 1.0, 0.0)
        kept = jnp.sum(hot, axis=1, keepdims=True) == 0.0
        hot = hot.astype(BF)
        raw = [
            jnp.where(kept, panel(k, j, slice(chunk_top, chunk)).astype(F32), dot(hot, far[k])) for k in range(2)
        ]
        first = dot_right(raw[0].astype(BF), upper_ref[0]).astype(BF)
        if j == 0:
            above = (lax.broadcasted_iota(jnp.int32, (block_rows, NB), 0) < NB) & (prow == 0)
            first = jnp.where(above, jnp.zeros_like(first), first)
        middle = (raw[1] - dot(first, top_mid)).astype(BF)
        second = dot_right(middle, upper_ref[1]).astype(BF)
        if j == 0:
            above = (lax.broadcasted_iota(jnp.int32, (block_rows, NB), 0) < NB) & (prow < 2)
            second = jnp.where(above, jnp.zeros_like(second), second)
        out_ref[j * block_rows:(j + 1) * block_rows, 0:NB] = first
        out_ref[j * block_rows:(j + 1) * block_rows, NB:] = second


def factor(where, index, mine, other, lower_inv, upper_inv, prow_count):
    rows_here = CHUNKS * (mine.shape[1] - SMALL // CHUNKS)
    smem = pl.BlockSpec(memory_space=pltpu.SMEM)
    vmem = pl.BlockSpec(memory_space=pltpu.VMEM)
    return pl.pallas_call(
        lambda *refs: factor_kernel(prow_count, *refs),
        out_shape=(jax.ShapeDtypeStruct((rows_here, TOP), BF), jax.ShapeDtypeStruct((NB, NB), BF)),
        in_specs=[smem] + [vmem] * 5,
        out_specs=(vmem, vmem),
        compiler_params=pltpu.CompilerParams(vmem_limit_bytes=VMEM_BYTES),
        name="factor",
    )(where, index.reshape(-1, NB), mine, other, lower_inv, upper_inv)


def update_kernel(prow_count, where_ref, index_ref, cols_ref, index_vec, *refs):
    parts = refs[:prow_count]
    low_ref, lower_ref, l_ref, matrix_ref, out_ref, a_ref, rows_ref, right, stages, sems, load_sems = refs[prow_count:]
    prow, pcol = where_ref[0], where_ref[1]
    steps, block_rows = STEPS, a_ref.shape[0] // STEPS
    slots = a_ref.shape[1] // NB
    lanes = lambda s: slice(s * NB, (s + 1) * NB)
    loads = []
    for step in range(steps):
        lines = pl.ds(step * block_rows, block_rows)
        loads.append(pltpu.make_async_copy(matrix_ref.at[lines, :], a_ref.at[lines, :], load_sems.at[step]))
        loads[step].start()
    top_part, old_part = TOP // prow_count, NB // prow_count
    for shift, part in enumerate(parts):
        source = lax.rem(prow + prow_count - shift, prow_count)
        rows_ref[pl.ds(pl.multiple_of(source * top_part, top_part), top_part), :] = part[0:top_part, :]
        for k in range(2):
            first = top_part + k * old_part
            line = pl.multiple_of(TOP + k * NB + source * old_part, old_part)
            right[pl.ds(line, old_part), :] = part[first:first + old_part, :]
    top = dot_left(lower_ref[0], rows_ref[0:NB, :]).astype(BF)
    for s in range(slots):
        block = cols_ref[pcol * slots + s]
        right[0:NB, lanes(s)] = jnp.where(block >= 1, -top[:, lanes(s)], jnp.zeros((NB, NB), BF))
    mid = (rows_ref[NB:TOP, :].astype(F32) + dot(low_ref[...], right[0:NB, :])).astype(BF)
    low = dot_left(lower_ref[1], mid).astype(BF)
    for s in range(slots):
        block = cols_ref[pcol * slots + s]
        right[NB:TOP, lanes(s)] = jnp.where(block >= 2, -low[:, lanes(s)], jnp.zeros((NB, NB), BF))

    dest = local_row(jnp.concatenate([index_vec[0:1, :], index_vec[1:2, :]], axis=1), prow, prow_count)
    copies = []
    for step in range(steps):
        lines = slice(step * block_rows, (step + 1) * block_rows)
        stage = stages.at[step % 2]
        if step >= 2:
            copies[step - 2].wait()
        loads[step].wait()
        line = lax.broadcasted_iota(jnp.int32, (block_rows, TOP), 0) + step * block_rows
        hot = jnp.where(line == dest, 1.0, 0.0)
        kept = jnp.sum(hot, axis=1, keepdims=True) == 0.0
        left = jnp.concatenate([l_ref[lines, :], hot.astype(BF)], axis=1)
        old = a_ref[lines, :].astype(F32)
        stage[...] = (jnp.where(kept, old, 0.0) + dot(left, right[...])).astype(BF)
        for k in range(2):
            slot = index_ref[TOP + k]

            @pl.when(slot // slots == pcol)
            def _():
                start = pl.multiple_of(slot % slots * NB, NB)
                stage[:, pl.ds(start, NB)] = l_ref[lines, k * NB:(k + 1) * NB]

        if step == 0:

            @pl.when(prow == 0)
            def _():
                for s in range(slots):
                    block = cols_ref[pcol * slots + s]
                    stage[0:NB, lanes(s)] = jnp.where(block >= 1, -right[0:NB, lanes(s)], rows_ref[0:NB, lanes(s)])

            @pl.when(prow == 1)
            def _():
                for s in range(slots):
                    block = cols_ref[pcol * slots + s]
                    changed = jnp.where(block == 1, mid[:, lanes(s)], -right[NB:TOP, lanes(s)])
                    stage[0:NB, lanes(s)] = jnp.where(block == 0, low_ref[...], changed)

        copies.append(pltpu.make_async_copy(stage, out_ref.at[pl.ds(step * block_rows, block_rows), :], sems.at[step % 2]))
        copies[step].start()
    for copy in copies[-2:]:
        copy.wait()


def update(where, index, col_blocks, parts, low, lower_inv, matrix, left, prow_count):
    rows_here, cols_here = matrix.shape
    smem = pl.BlockSpec(memory_space=pltpu.SMEM)
    vmem = pl.BlockSpec(memory_space=pltpu.VMEM)
    return pl.pallas_call(
        lambda *refs: update_kernel(prow_count, *refs),
        out_shape=jax.ShapeDtypeStruct(matrix.shape, BF),
        in_specs=[smem] * 3 + [vmem] * (1 + prow_count + 3) + [pl.BlockSpec(memory_space=pltpu.HBM)],
        out_specs=pl.BlockSpec(memory_space=pltpu.HBM),
        scratch_shapes=[
            pltpu.VMEM(matrix.shape, BF),
            pltpu.VMEM((TOP, cols_here), BF),
            pltpu.VMEM((2 * TOP, cols_here), BF),
            pltpu.VMEM((2, rows_here // STEPS, cols_here), BF),
            pltpu.SemaphoreType.DMA((2,)),
            pltpu.SemaphoreType.DMA((STEPS,)),
        ],
        compiler_params=pltpu.CompilerParams(vmem_limit_bytes=VMEM_BYTES),
        name="update",
    )(where, index, col_blocks, index.reshape(-1, NB), *parts, low, lower_inv, left, matrix)


CORE_SWAP = [(i, i ^ 1) for i in range(PY * PX * CORES)]
Y_GROUPS = [[(y * PX + x) * CORES + c for y in range(PY)] for x in range(PX) for c in range(CORES)]
X_GROUPS = [[(y * PX + x) * CORES + c for x in range(PX)] for y in range(PY) for c in range(CORES)]


def spread(x, axis, groups, count):
    x = jnp.broadcast_to(x[None], (count,) + x.shape)
    return lax.all_to_all(x, axis, 0, 0, axis_index_groups=groups)


def local(matrix, pivots, col_blocks, lower_inv, upper_inv):
    prow_count = lax.axis_size("prow")
    prow = lax.axis_index("prow")
    pcol = lax.axis_index("pcol")
    core = pcol % CORES
    where = jnp.stack([prow, pcol, core]).astype(jnp.int32)
    slots = matrix.shape[1] // NB

    top = jnp.arange(TOP, dtype=jnp.int32)
    meta = jnp.concatenate([pivots.reshape(-1), col_blocks, top, top])
    index, parts, own, send = fetch(where, meta, matrix, prow_count)
    barrier = lax.optimization_barrier
    ups = [(i, (i + 1) % prow_count) for i in range(prow_count)]
    downs = [(i, (i - 1) % prow_count) for i in range(prow_count)]

    def part_at(offset):
        return lax.dynamic_index_in_dim(parts, (prow + offset) % prow_count, 0, keepdims=False)

    def go_up(x, step):
        return lax.ppermute(x, "prow", ups) + part_at(4 - step)

    def go_down(x, step):
        x = lax.ppermute(x, "prow", downs)
        return x + part_at(step - 3) if step < 3 else x

    got = {}

    def gather_step(step):
        got[step] = lax.ppermute(got[step - 1], "prow", ups)
        if step < 4:
            got[prow_count - step] = lax.ppermute(got[(prow_count - step + 1) % prow_count], "prow", downs)

    state = {}

    def ring(names):
        for name in names.split():
            kind, step = name[0], int(name[1])
            if kind == "U":
                state["up"] = go_up(state["up"] if step > 1 else part_at(4), step)
            elif kind == "D":
                state["down"] = go_down(state["down"] if step > 1 else part_at(-3), step)
            elif kind == "G":
                if step == 1:
                    got[0] = state.pop("up") + state.pop("down")
                gather_step(step)

    def fence(panel, extra=()):
        flat, tree = jax.tree.flatten((panel, dict(got), dict(state), extra))
        panel, now, then, extra = jax.tree.unflatten(tree, barrier(flat))
        got.update(now)
        state.update(then)
        return panel, extra

    windows = PLAN.split("|")
    owner = lax.dynamic_index_in_dim(index[TOP:TOP + 2], core, 0, keepdims=False) // slots
    chip_y, chip_x = owner // (CORES * PX), owner // CORES % PX
    chunk_top = SMALL // CHUNKS
    ring(windows[0])
    panel = own + lax.ppermute(send, "pcol", CORE_SWAP)
    panel = lax.all_to_all(panel, "pcol", 0, 0, axis_index_groups=Y_GROUPS)
    ring(windows[1])
    panel, (chip_y, chip_x) = fence(panel, (chip_y, chip_x))

    panel = lax.dynamic_index_in_dim(panel, chip_y, 0, keepdims=False)
    small = jnp.sum(spread(panel[:chunk_top], "prow", None, prow_count), axis=0, dtype=BF)
    panel = jnp.concatenate([small, panel[chunk_top:]], axis=0)
    ring(windows[2])
    panel, _ = fence(panel)

    panel = spread(panel, "pcol", X_GROUPS, PX)
    ring(windows[3])
    panel, _ = fence(panel)

    panel = lax.dynamic_index_in_dim(panel, chip_x, 0, keepdims=False)
    mine = spread(panel, "pcol", Y_GROUPS, PY)
    ring(windows[4])
    mine, _ = fence(mine)
    ring(windows[5])
    other = lax.ppermute(mine, "pcol", CORE_SWAP)

    left, low = factor(where, index, mine, other, lower_inv, upper_inv, prow_count)
    return update(where, index, col_blocks, [got[s] for s in range(prow_count)], low, lower_inv, matrix, left, prow_count)


def solution(mesh):
    in_specs = (P("prow", "pcol"), P(), P(), P(), P())
    out_specs = P("prow", "pcol")
    return jax.shard_map(local, mesh=mesh, in_specs=in_specs, out_specs=out_specs, check_vma=False)
```

```python
import jax
import jax.numpy as jnp
from jax import lax
from jax.experimental import pallas as pl
from jax.experimental.pallas import tpu as pltpu
from jax.sharding import PartitionSpec as P

NB = 128
TOP = 2 * NB
PY, PX, CORES = 4, 4, 2
CHUNKS = PY * PX
SMALL = 4 * NB
STEPS = 6
PLAN = ("U1 D1", "U2 D2 U3 D3", "U4 G1", "G2 G3", "G4")
VMEM_BYTES = 50 * 1024 * 1024

BF = jnp.bfloat16
F32 = jnp.float32


def split3(x):
    high = x.astype(BF)
    rest = x - high.astype(F32)
    mid = rest.astype(BF)
    low = (rest - mid.astype(F32)).astype(BF)
    return high, mid, low


def dot(a, b):
    return jnp.dot(a, b, preferred_element_type=F32)


def dot_right(x, w):
    high, mid, low = split3(w)
    return dot(x, low) + dot(x, mid) + dot(x, high)


def dot_left(w, x):
    high, mid, low = split3(w)
    return dot(low, x) + dot(mid, x) + dot(high, x)


def local_row(rows, prow, prow_count):
    here = (rows // NB) % prow_count == prow
    return jnp.where(here & (rows >= 0), rows // (NB * prow_count) * NB + rows % NB, -1)


def fetch_kernel(where_ref, meta_ref, a_ref, index_ref, parts_ref, own_ref, send_ref, order, piv_ref, held, slab, picked, old, sems, panel_sems, top_sems):
    prow, core = where_ref[0], where_ref[2]
    prow_count = parts_ref.shape[0]
    slots = a_ref.shape[1] // NB
    chunk_top = SMALL // CHUNKS
    block_rows = a_ref.shape[0] // CHUNKS
    top_part, old_part = TOP // prow_count, NB // prow_count
    piv_copy = pltpu.make_async_copy(meta_ref.at[pl.ds(0, 2), :], piv_ref, top_sems.at[0])
    old_copy = pltpu.make_async_copy(a_ref.at[pl.ds(0, NB), :], old, top_sems.at[1])
    piv_copy.start()
    old_copy.start()
    at = lax.broadcasted_iota(jnp.int32, (2, NB), 0) * NB + lax.broadcasted_iota(jnp.int32, (2, NB), 1)
    places = [
        jnp.sum(jnp.where(meta_ref[2:4, :] == k, at, 0).astype(F32)).astype(jnp.int32) for k in range(2)
    ]
    panels = []
    for n, (out, panel) in enumerate(((own_ref, core), (send_ref, 1 - core))):
        place = jnp.where(panel == 0, places[0], places[1])
        start = pl.multiple_of(place % slots * NB, NB)
        copies = [
            pltpu.make_async_copy(
                a_ref.at[pl.ds(j * block_rows, block_rows), pl.ds(start, NB)],
                out.at[j, pl.ds(chunk_top, block_rows), :],
                panel_sems.at[n, j],
            )
            for j in range(CHUNKS)
        ]
        panels.append((out, panel, start, place // slots % CORES == core, copies))

        @pl.when(panels[n][3])
        def _():
            for copy in copies:
                copy.start()

    for k in range(2):
        index_ref[TOP + k] = places[k]

    def init(t, carry):
        order[t] = t
        index_ref[t] = -1
        return carry

    lax.fori_loop(0, TOP, init, 0, unroll=TOP)
    piv_copy.wait()

    def untouched(t):
        far = piv_ref[t // NB, t % NB]
        order[far] = far

    for t in range(TOP):
        untouched(t)

    def exchange(t):
        far = piv_ref[t // NB, t % NB]
        near_value = order[t]
        far_value = order[far]
        order[t] = far_value
        order[far] = near_value

    for t in range(TOP):
        exchange(t)

    def collect(g, count):
        held[count] = g
        return count + ((order[g] >> 7) & (prow_count - 1) == prow).astype(jnp.int32)

    count = lax.fori_loop(0, TOP, collect, 0, unroll=TOP)

    def line_of(n):
        row = order[held[n]]
        return (row >> 10) * NB + (row & (NB - 1))

    def slab_copy(n, line):
        first = pl.multiple_of(line >> 4 << 4, 16)
        return pltpu.make_async_copy(a_ref.at[pl.ds(first, 16), :], slab.at[n], sems.at[n])

    def begin(n, carry):
        slab_copy(n, line_of(n)).start()
        return carry

    lax.fori_loop(0, count, begin, 0)
    picked[...] = jnp.zeros_like(picked)

    def emit(t):
        far = piv_ref[t // NB, t % NB]
        index_ref[jnp.where(far >= TOP, order[far], TOP + NB)] = far

    for t in range(TOP):
        emit(t)
    line16 = lax.broadcasted_iota(jnp.int32, (16, a_ref.shape[1]), 0)

    def take(n, carry):
        line = line_of(n)
        slab_copy(n, line).wait()
        chosen = jnp.where(line16 == (line & 15), slab[n].astype(F32), 0.0)
        picked[pl.ds(held[n], 1), :] = jnp.sum(chosen, axis=0, keepdims=True)
        return carry

    lax.fori_loop(0, count, take, 0)
    old_copy.wait()
    for q in range(prow_count):
        parts_ref[q, 0:top_part, :] = picked[q * top_part:(q + 1) * top_part, :].astype(BF)
        for k in range(2):
            first = top_part + k * old_part
            mine = old[q * old_part:(q + 1) * old_part, :]
            parts_ref[q, first:first + old_part, :] = jnp.where(prow == k, mine, jnp.zeros_like(mine))
    for out, panel, start, valid, copies in panels:

        @pl.when(valid)
        def _():
            near = picked[pl.ds(pl.multiple_of((1 - panel) * NB, NB), NB), pl.ds(start, NB)].astype(BF)
            far = old[:, pl.ds(start, NB)]
            zero = jnp.zeros_like(far)
            small = jnp.concatenate([near, jnp.where(prow == 0, far, zero), jnp.where(prow == 1, far, zero), zero], axis=0)
            for copy in copies:
                copy.wait()
            for j in range(CHUNKS):
                out[j, 0:chunk_top, :] = small[j * chunk_top:(j + 1) * chunk_top]

        @pl.when(jnp.logical_not(valid))
        def _():
            out[...] = jnp.zeros_like(out)


def fetch(where, meta, matrix, prow_count):
    rows_here, cols_here = matrix.shape
    chunk = (rows_here + SMALL) // CHUNKS
    part = 2 * TOP // prow_count
    smem = pl.BlockSpec(memory_space=pltpu.SMEM)
    vmem = pl.BlockSpec(memory_space=pltpu.VMEM)
    hbm = pl.BlockSpec(memory_space=pltpu.HBM)
    return pl.pallas_call(
        fetch_kernel,
        out_shape=(
            jax.ShapeDtypeStruct((2 * TOP,), jnp.int32),
            jax.ShapeDtypeStruct((prow_count, part, cols_here), BF),
            jax.ShapeDtypeStruct((CHUNKS, chunk, NB), BF),
            jax.ShapeDtypeStruct((CHUNKS, chunk, NB), BF),
        ),
        in_specs=[smem, vmem, hbm],
        out_specs=(smem, vmem, vmem, vmem),
        scratch_shapes=[
            pltpu.SMEM((rows_here * prow_count,), jnp.int32),
            pltpu.SMEM((2, NB), jnp.int32),
            pltpu.SMEM((TOP + 1,), jnp.int32),
            pltpu.VMEM((TOP, 16, cols_here), BF),
            pltpu.VMEM((TOP, cols_here), F32),
            pltpu.VMEM((NB, cols_here), BF),
            pltpu.SemaphoreType.DMA((TOP,)),
            pltpu.SemaphoreType.DMA((2, CHUNKS)),
            pltpu.SemaphoreType.DMA((2,)),
        ],
        compiler_params=pltpu.CompilerParams(vmem_limit_bytes=VMEM_BYTES),
        name="fetch",
    )(where, meta, matrix)


def factor_kernel(prow_count, where_ref, index_vec, mine_ref, other_ref, lower_ref, upper_ref, out_ref, low_ref):
    prow, core = where_ref[0], where_ref[2]
    chunk = mine_ref.shape[1]
    chunk_top = SMALL // CHUNKS
    block_rows = chunk - chunk_top

    def panel(k, j, part):
        mine, other = mine_ref[j, part, :], other_ref[j, part, :]
        return jnp.where(core == k, mine, other)

    small = [jnp.concatenate([panel(k, j, slice(0, chunk_top)) for j in range(CHUNKS)], axis=0) for k in range(2)]
    near_mid, near_top = small[0][0:NB], small[1][0:NB]
    far = [small[0][NB:NB + TOP], small[1][NB:NB + TOP]]
    top_mid = dot_left(lower_ref[0], near_top).astype(BF)
    low_ref[...] = dot_right(near_mid, upper_ref[0]).astype(BF)
    dest = local_row(jnp.concatenate([index_vec[0:1, :], index_vec[1:2, :]], axis=1), prow, prow_count)
    group = CHUNKS // PY
    block_rows *= group
    for j in range(PY):
        line = lax.broadcasted_iota(jnp.int32, (block_rows, TOP), 0) + j * block_rows
        hot = jnp.where(line == dest, 1.0, 0.0)
        kept = jnp.sum(hot, axis=1, keepdims=True) == 0.0
        hot = hot.astype(BF)
        raw = []
        for k in range(2):
            here = jnp.concatenate([panel(k, j * group + i, slice(chunk_top, chunk)) for i in range(group)], axis=0)
            raw.append(jnp.where(kept, here.astype(F32), dot(hot, far[k])))
        first = dot_right(raw[0].astype(BF), upper_ref[0]).astype(BF)
        if j == 0:
            above = (lax.broadcasted_iota(jnp.int32, (block_rows, NB), 0) < NB) & (prow == 0)
            first = jnp.where(above, jnp.zeros_like(first), first)
        middle = (raw[1] - dot(first, top_mid)).astype(BF)
        second = dot_right(middle, upper_ref[1]).astype(BF)
        if j == 0:
            above = (lax.broadcasted_iota(jnp.int32, (block_rows, NB), 0) < NB) & (prow < 2)
            second = jnp.where(above, jnp.zeros_like(second), second)
        out_ref[j * block_rows:(j + 1) * block_rows, 0:NB] = first
        out_ref[j * block_rows:(j + 1) * block_rows, NB:] = second


def factor(where, index, mine, other, lower_inv, upper_inv, prow_count):
    rows_here = CHUNKS * (mine.shape[1] - SMALL // CHUNKS)
    smem = pl.BlockSpec(memory_space=pltpu.SMEM)
    vmem = pl.BlockSpec(memory_space=pltpu.VMEM)
    return pl.pallas_call(
        lambda *refs: factor_kernel(prow_count, *refs),
        out_shape=(jax.ShapeDtypeStruct((rows_here, TOP), BF), jax.ShapeDtypeStruct((NB, NB), BF)),
        in_specs=[smem] + [vmem] * 5,
        out_specs=(vmem, vmem),
        compiler_params=pltpu.CompilerParams(vmem_limit_bytes=VMEM_BYTES),
        name="factor",
    )(where, index.reshape(-1, NB), mine, other, lower_inv, upper_inv)


def update_kernel(prow_count, where_ref, index_ref, cols_ref, index_vec, *refs):
    parts = refs[:prow_count]
    low_ref, lower_ref, l_ref, matrix_ref, out_ref, a_ref, rows_ref, right, stages, sems, load_sems = refs[prow_count:]
    prow, pcol = where_ref[0], where_ref[1]
    steps, block_rows = STEPS, a_ref.shape[0] // STEPS
    slots = a_ref.shape[1] // NB
    lanes = lambda s: slice(s * NB, (s + 1) * NB)
    loads = []
    for step in range(steps):
        lines = pl.ds(step * block_rows, block_rows)
        loads.append(pltpu.make_async_copy(matrix_ref.at[lines, :], a_ref.at[lines, :], load_sems.at[step]))
        loads[step].start()
    top_part, old_part = TOP // prow_count, NB // prow_count
    for shift, part in enumerate(parts):
        source = lax.rem(prow + prow_count - shift, prow_count)
        rows_ref[pl.ds(pl.multiple_of(source * top_part, top_part), top_part), :] = part[0:top_part, :]
        for k in range(2):
            first = top_part + k * old_part
            line = pl.multiple_of(TOP + k * NB + source * old_part, old_part)
            right[pl.ds(line, old_part), :] = part[first:first + old_part, :]
    top = dot_left(lower_ref[0], rows_ref[0:NB, :]).astype(BF)
    for s in range(slots):
        block = cols_ref[pcol * slots + s]
        right[0:NB, lanes(s)] = jnp.where(block >= 1, -top[:, lanes(s)], jnp.zeros((NB, NB), BF))
    mid = (rows_ref[NB:TOP, :].astype(F32) + dot(low_ref[...], right[0:NB, :])).astype(BF)
    low = dot_left(lower_ref[1], mid).astype(BF)
    for s in range(slots):
        block = cols_ref[pcol * slots + s]
        right[NB:TOP, lanes(s)] = jnp.where(block >= 2, -low[:, lanes(s)], jnp.zeros((NB, NB), BF))

    dest = local_row(jnp.concatenate([index_vec[0:1, :], index_vec[1:2, :]], axis=1), prow, prow_count)
    copies = []
    for step in range(steps):
        lines = slice(step * block_rows, (step + 1) * block_rows)
        stage = stages.at[step % 2]
        if step >= 2:
            copies[step - 2].wait()
        loads[step].wait()
        line = lax.broadcasted_iota(jnp.int32, (block_rows, TOP), 0) + step * block_rows
        hot = jnp.where(line == dest, 1.0, 0.0)
        kept = jnp.sum(hot, axis=1, keepdims=True) == 0.0
        left = jnp.concatenate([l_ref[lines, :], hot.astype(BF)], axis=1)
        old = a_ref[lines, :].astype(F32)
        stage[...] = (jnp.where(kept, old, 0.0) + dot(left, right[...])).astype(BF)
        for k in range(2):
            slot = index_ref[TOP + k]

            @pl.when(slot // slots == pcol)
            def _():
                start = pl.multiple_of(slot % slots * NB, NB)
                stage[:, pl.ds(start, NB)] = l_ref[lines, k * NB:(k + 1) * NB]

        if step == 0:

            @pl.when(prow == 0)
            def _():
                for s in range(slots):
                    block = cols_ref[pcol * slots + s]
                    stage[0:NB, lanes(s)] = jnp.where(block >= 1, -right[0:NB, lanes(s)], rows_ref[0:NB, lanes(s)])

            @pl.when(prow == 1)
            def _():
                for s in range(slots):
                    block = cols_ref[pcol * slots + s]
                    changed = jnp.where(block == 1, mid[:, lanes(s)], -right[NB:TOP, lanes(s)])
                    stage[0:NB, lanes(s)] = jnp.where(block == 0, low_ref[...], changed)

        copies.append(pltpu.make_async_copy(stage, out_ref.at[pl.ds(step * block_rows, block_rows), :], sems.at[step % 2]))
        copies[step].start()
    for copy in copies[-2:]:
        copy.wait()


def update(where, index, col_blocks, parts, low, lower_inv, matrix, left, prow_count):
    rows_here, cols_here = matrix.shape
    smem = pl.BlockSpec(memory_space=pltpu.SMEM)
    vmem = pl.BlockSpec(memory_space=pltpu.VMEM)
    return pl.pallas_call(
        lambda *refs: update_kernel(prow_count, *refs),
        out_shape=jax.ShapeDtypeStruct(matrix.shape, BF),
        in_specs=[smem] * 3 + [vmem] * (1 + prow_count + 3) + [pl.BlockSpec(memory_space=pltpu.HBM)],
        out_specs=pl.BlockSpec(memory_space=pltpu.HBM),
        scratch_shapes=[
            pltpu.VMEM(matrix.shape, BF),
            pltpu.VMEM((TOP, cols_here), BF),
            pltpu.VMEM((2 * TOP, cols_here), BF),
            pltpu.VMEM((2, rows_here // STEPS, cols_here), BF),
            pltpu.SemaphoreType.DMA((2,)),
            pltpu.SemaphoreType.DMA((STEPS,)),
        ],
        compiler_params=pltpu.CompilerParams(vmem_limit_bytes=VMEM_BYTES),
        name="update",
    )(where, index, col_blocks, index.reshape(-1, NB), *parts, low, lower_inv, left, matrix)


CORE_SWAP = [(i, i ^ 1) for i in range(PY * PX * CORES)]
CHIP_GROUPS = [[i * CORES + c for i in range(PY * PX)] for c in range(CORES)]


def spread(x, axis, groups, count):
    x = jnp.broadcast_to(x[None], (count,) + x.shape)
    return lax.all_to_all(x, axis, 0, 0, axis_index_groups=groups)


def local(matrix, pivots, col_blocks, lower_inv, upper_inv):
    prow_count = lax.axis_size("prow")
    prow = lax.axis_index("prow")
    pcol = lax.axis_index("pcol")
    core = pcol % CORES
    where = jnp.stack([prow, pcol, core]).astype(jnp.int32)
    slots = matrix.shape[1] // NB

    meta = jnp.concatenate([pivots, col_blocks.reshape(-1, NB)], axis=0)
    index, parts, own, send = fetch(where, meta, matrix, prow_count)
    barrier = lax.optimization_barrier
    ups = [(i, (i + 1) % prow_count) for i in range(prow_count)]
    downs = [(i, (i - 1) % prow_count) for i in range(prow_count)]

    def part_at(offset):
        return lax.dynamic_index_in_dim(parts, (prow + offset) % prow_count, 0, keepdims=False)

    def go_up(x, step):
        x = lax.ppermute(x, "prow", ups)
        if step == 1:
            x, _ = barrier((x, panel))
        return x + part_at(4 - step)

    def go_down(x, step):
        x = lax.ppermute(x, "prow", downs)
        return x + part_at(step - 3) if step < 3 else x

    got = {}

    def gather_step(step):
        got[step] = lax.ppermute(got[step - 1], "prow", ups)
        if step < 4:
            got[prow_count - step] = lax.ppermute(got[(prow_count - step + 1) % prow_count], "prow", downs)

    state = {}

    def ring(names):
        for name in names.split():
            kind, step = name[0], int(name[1])
            if kind == "U":
                state["up"] = go_up(state["up"] if step > 1 else part_at(4), step)
            elif kind == "D":
                state["down"] = go_down(state["down"] if step > 1 else part_at(-3), step)
            elif kind == "G":
                if step == 1:
                    got[0] = state.pop("up") + state.pop("down")
                gather_step(step)

    def fence(panel, extra=()):
        flat, tree = jax.tree.flatten((panel, dict(got), dict(state), extra))
        panel, now, then, extra = jax.tree.unflatten(tree, barrier(flat))
        got.update(now)
        state.update(then)
        return panel, extra

    owner = lax.dynamic_index_in_dim(index[TOP:TOP + 2], core, 0, keepdims=False) // slots
    chip = owner // CORES
    chunk_top = SMALL // CHUNKS
    panel = own + lax.ppermute(send, "pcol", CORE_SWAP)
    ring(PLAN[0])
    panel = lax.all_to_all(panel, "pcol", 0, 0, axis_index_groups=CHIP_GROUPS)
    ring(PLAN[1])
    panel, chip = fence(panel, chip)

    panel = lax.dynamic_index_in_dim(panel, chip, 0, keepdims=False)
    small = jnp.sum(spread(panel[:chunk_top], "prow", None, prow_count), axis=0, dtype=BF)
    panel = jnp.concatenate([small, panel[chunk_top:]], axis=0)
    ring(PLAN[2])
    panel, _ = fence(panel)

    mine = spread(panel, "pcol", CHIP_GROUPS, CHUNKS)
    ring(PLAN[3])
    mine, _ = fence(mine)
    ring(PLAN[4])
    other = lax.ppermute(mine, "pcol", CORE_SWAP)

    left, low = factor(where, index, mine, other, lower_inv, upper_inv, prow_count)
    return update(where, index, col_blocks, [got[s] for s in range(prow_count)], low, lower_inv, matrix, left, prow_count)


def solution(mesh):
    in_specs = (P("prow", "pcol"), P(), P(), P(), P())
    out_specs = P("prow", "pcol")
    return jax.shard_map(local, mesh=mesh, in_specs=in_specs, out_specs=out_specs, check_vma=False)
```

```python
import jax
import jax.numpy as jnp
from jax import lax
from jax.experimental import pallas as pl
from jax.experimental.pallas import tpu as pltpu
from jax.sharding import PartitionSpec as P

NB = 128
TOP = 2 * NB
PY, PX, CORES = 4, 4, 2
CHUNKS = PY * PX
SMALL = 4 * NB
STEPS = 4
PLAN = ("D1 U1", "D2 U2 D3 U3", "U4 G1", "G2 G3", "G4")
VMEM_BYTES = 50 * 1024 * 1024

BF = jnp.bfloat16
F32 = jnp.float32


def split3(x):
    high = x.astype(BF)
    rest = x - high.astype(F32)
    mid = rest.astype(BF)
    low = (rest - mid.astype(F32)).astype(BF)
    return high, mid, low


def dot(a, b):
    return jnp.dot(a, b, preferred_element_type=F32)


def dot_right(x, w):
    high, mid, low = split3(w)
    return dot(x, low) + dot(x, mid) + dot(x, high)


def dot_left(w, x):
    high, mid, low = split3(w)
    return dot(low, x) + dot(mid, x) + dot(high, x)


def local_row(rows, prow, prow_count):
    here = (rows // NB) % prow_count == prow
    return jnp.where(here & (rows >= 0), rows // (NB * prow_count) * NB + rows % NB, -1)


def fetch_kernel(where_ref, meta_ref, a_ref, index_ref, parts_ref, own_ref, send_ref, order, piv_ref, held, slab, picked, old, sems, panel_sems, top_sems):
    prow, core = where_ref[0], where_ref[2]
    prow_count = parts_ref.shape[0]
    slots = a_ref.shape[1] // NB
    chunk_top = SMALL // CHUNKS
    block_rows = a_ref.shape[0] // CHUNKS
    top_part, old_part = TOP // prow_count, NB // prow_count
    piv_copy = pltpu.make_async_copy(meta_ref.at[pl.ds(0, 2), :], piv_ref, top_sems.at[0])
    old_copy = pltpu.make_async_copy(a_ref.at[pl.ds(0, NB), :], old, top_sems.at[1])
    piv_copy.start()
    old_copy.start()
    at = lax.broadcasted_iota(jnp.int32, (2, NB), 0) * NB + lax.broadcasted_iota(jnp.int32, (2, NB), 1)
    places = [
        jnp.sum(jnp.where(meta_ref[2:4, :] == k, at, 0).astype(F32)).astype(jnp.int32) for k in range(2)
    ]
    panels = []
    for n, (out, panel) in enumerate(((own_ref, core), (send_ref, 1 - core))):
        place = jnp.where(panel == 0, places[0], places[1])
        start = pl.multiple_of(place % slots * NB, NB)
        copies = [
            pltpu.make_async_copy(
                a_ref.at[pl.ds(j * block_rows, block_rows), pl.ds(start, NB)],
                out.at[j, pl.ds(chunk_top, block_rows), :],
                panel_sems.at[n, j],
            )
            for j in range(CHUNKS)
        ]
        panels.append((out, panel, start, place // slots % CORES == core, copies))

        @pl.when(panels[n][3])
        def _():
            for copy in copies:
                copy.start()

    for k in range(2):
        index_ref[TOP + k] = places[k]

    def init(t, carry):
        order[t] = t
        index_ref[t] = -1
        return carry

    lax.fori_loop(0, TOP, init, 0, unroll=TOP)
    piv_copy.wait()

    def untouched(t):
        far = piv_ref[t // NB, t % NB]
        order[far] = far

    for t in range(TOP):
        untouched(t)

    def exchange(t):
        far = piv_ref[t // NB, t % NB]
        near_value = order[t]
        far_value = order[far]
        order[t] = far_value
        order[far] = near_value

    for t in range(TOP):
        exchange(t)

    def collect(g, count):
        held[count] = g
        return count + ((order[g] >> 7) & (prow_count - 1) == prow).astype(jnp.int32)

    count = lax.fori_loop(0, TOP, collect, 0, unroll=TOP)

    def line_of(n):
        row = order[held[n]]
        return (row >> 10) * NB + (row & (NB - 1))

    def slab_copy(n, line):
        first = pl.multiple_of(line >> 4 << 4, 16)
        return pltpu.make_async_copy(a_ref.at[pl.ds(first, 16), :], slab.at[n], sems.at[n])

    def begin(n, carry):
        slab_copy(n, line_of(n)).start()
        return carry

    lax.fori_loop(0, count, begin, 0)
    picked[...] = jnp.zeros_like(picked)

    def emit(t):
        far = piv_ref[t // NB, t % NB]
        index_ref[jnp.where(far >= TOP, order[far], TOP + NB)] = far

    for t in range(TOP):
        emit(t)
    line16 = lax.broadcasted_iota(jnp.int32, (16, a_ref.shape[1]), 0)

    def take(n, carry):
        line = line_of(n)
        slab_copy(n, line).wait()
        chosen = jnp.where(line16 == (line & 15), slab[n].astype(F32), 0.0)
        picked[pl.ds(held[n], 1), :] = jnp.sum(chosen, axis=0, keepdims=True)
        return carry

    lax.fori_loop(0, count, take, 0)
    old_copy.wait()
    for q in range(prow_count):
        parts_ref[q, 0:top_part, :] = picked[q * top_part:(q + 1) * top_part, :].astype(BF)
        for k in range(2):
            first = top_part + k * old_part
            mine = old[q * old_part:(q + 1) * old_part, :]
            parts_ref[q, first:first + old_part, :] = jnp.where(prow == k, mine, jnp.zeros_like(mine))
    for out, panel, start, valid, copies in panels:

        @pl.when(valid)
        def _():
            near = picked[pl.ds(pl.multiple_of((1 - panel) * NB, NB), NB), pl.ds(start, NB)].astype(BF)
            far = old[:, pl.ds(start, NB)]
            zero = jnp.zeros_like(far)
            small = jnp.concatenate([near, jnp.where(prow == 0, far, zero), jnp.where(prow == 1, far, zero), zero], axis=0)
            for copy in copies:
                copy.wait()
            for j in range(CHUNKS):
                out[j, 0:chunk_top, :] = small[j * chunk_top:(j + 1) * chunk_top]

        @pl.when(jnp.logical_not(valid))
        def _():
            out[...] = jnp.zeros_like(out)


def fetch(where, meta, matrix, prow_count):
    rows_here, cols_here = matrix.shape
    chunk = (rows_here + SMALL) // CHUNKS
    part = 2 * TOP // prow_count
    smem = pl.BlockSpec(memory_space=pltpu.SMEM)
    vmem = pl.BlockSpec(memory_space=pltpu.VMEM)
    hbm = pl.BlockSpec(memory_space=pltpu.HBM)
    return pl.pallas_call(
        fetch_kernel,
        out_shape=(
            jax.ShapeDtypeStruct((2 * TOP,), jnp.int32),
            jax.ShapeDtypeStruct((prow_count, part, cols_here), BF),
            jax.ShapeDtypeStruct((CHUNKS, chunk, NB), BF),
            jax.ShapeDtypeStruct((CHUNKS, chunk, NB), BF),
        ),
        in_specs=[smem, vmem, hbm],
        out_specs=(smem, vmem, vmem, vmem),
        scratch_shapes=[
            pltpu.SMEM((rows_here * prow_count,), jnp.int32),
            pltpu.SMEM((2, NB), jnp.int32),
            pltpu.SMEM((TOP + 1,), jnp.int32),
            pltpu.VMEM((TOP, 16, cols_here), BF),
            pltpu.VMEM((TOP, cols_here), F32),
            pltpu.VMEM((NB, cols_here), BF),
            pltpu.SemaphoreType.DMA((TOP,)),
            pltpu.SemaphoreType.DMA((2, CHUNKS)),
            pltpu.SemaphoreType.DMA((2,)),
        ],
        compiler_params=pltpu.CompilerParams(vmem_limit_bytes=VMEM_BYTES),
        name="fetch",
    )(where, meta, matrix)


def factor_kernel(prow_count, where_ref, index_vec, mine_ref, other_ref, lower_ref, upper_ref, out_ref, low_ref):
    prow, core = where_ref[0], where_ref[2]
    chunk = mine_ref.shape[1]
    chunk_top = SMALL // CHUNKS
    block_rows = chunk - chunk_top

    def panel(k, j, part):
        mine, other = mine_ref[j, part, :], other_ref[j, part, :]
        return jnp.where(core == k, mine, other)

    small = [jnp.concatenate([panel(k, j, slice(0, chunk_top)) for j in range(CHUNKS)], axis=0) for k in range(2)]
    near_mid, near_top = small[0][0:NB], small[1][0:NB]
    far = [small[0][NB:NB + TOP], small[1][NB:NB + TOP]]
    top_mid = dot_left(lower_ref[0], near_top).astype(BF)
    low_ref[...] = dot_right(near_mid, upper_ref[0]).astype(BF)
    dest = local_row(jnp.concatenate([index_vec[0:1, :], index_vec[1:2, :]], axis=1), prow, prow_count)
    group = CHUNKS // PY
    block_rows *= group
    for j in range(PY):
        line = lax.broadcasted_iota(jnp.int32, (block_rows, TOP), 0) + j * block_rows
        hot = jnp.where(line == dest, 1.0, 0.0)
        kept = jnp.sum(hot, axis=1, keepdims=True) == 0.0
        hot = hot.astype(BF)
        raw = []
        for k in range(2):
            here = jnp.concatenate([panel(k, j * group + i, slice(chunk_top, chunk)) for i in range(group)], axis=0)
            raw.append(jnp.where(kept, here.astype(F32), dot(hot, far[k])))
        first = dot_right(raw[0].astype(BF), upper_ref[0]).astype(BF)
        if j == 0:
            above = (lax.broadcasted_iota(jnp.int32, (block_rows, NB), 0) < NB) & (prow == 0)
            first = jnp.where(above, jnp.zeros_like(first), first)
        middle = (raw[1] - dot(first, top_mid)).astype(BF)
        second = dot_right(middle, upper_ref[1]).astype(BF)
        if j == 0:
            above = (lax.broadcasted_iota(jnp.int32, (block_rows, NB), 0) < NB) & (prow < 2)
            second = jnp.where(above, jnp.zeros_like(second), second)
        out_ref[j * block_rows:(j + 1) * block_rows, 0:NB] = first
        out_ref[j * block_rows:(j + 1) * block_rows, NB:] = second


def factor(where, index, mine, other, lower_inv, upper_inv, prow_count):
    rows_here = CHUNKS * (mine.shape[1] - SMALL // CHUNKS)
    smem = pl.BlockSpec(memory_space=pltpu.SMEM)
    vmem = pl.BlockSpec(memory_space=pltpu.VMEM)
    return pl.pallas_call(
        lambda *refs: factor_kernel(prow_count, *refs),
        out_shape=(jax.ShapeDtypeStruct((rows_here, TOP), BF), jax.ShapeDtypeStruct((NB, NB), BF)),
        in_specs=[smem] + [vmem] * 5,
        out_specs=(vmem, vmem),
        compiler_params=pltpu.CompilerParams(vmem_limit_bytes=VMEM_BYTES),
        name="factor",
    )(where, index.reshape(-1, NB), mine, other, lower_inv, upper_inv)


def update_kernel(prow_count, where_ref, index_ref, cols_ref, index_vec, *refs):
    parts = refs[:prow_count]
    low_ref, lower_ref, l_ref, matrix_ref, out_ref, a_ref, rows_ref, right, stages, sems, load_sems = refs[prow_count:]
    prow, pcol = where_ref[0], where_ref[1]
    steps, block_rows = STEPS, a_ref.shape[0] // STEPS
    slots = a_ref.shape[1] // NB
    lanes = lambda s: slice(s * NB, (s + 1) * NB)
    loads = []
    for step in range(steps):
        lines = pl.ds(step * block_rows, block_rows)
        loads.append(pltpu.make_async_copy(matrix_ref.at[lines, :], a_ref.at[lines, :], load_sems.at[step]))
        loads[step].start()
    top_part, old_part = TOP // prow_count, NB // prow_count
    for shift, part in enumerate(parts):
        source = lax.rem(prow + prow_count - shift, prow_count)
        rows_ref[pl.ds(pl.multiple_of(source * top_part, top_part), top_part), :] = part[0:top_part, :]
        for k in range(2):
            first = top_part + k * old_part
            line = pl.multiple_of(TOP + k * NB + source * old_part, old_part)
            right[pl.ds(line, old_part), :] = part[first:first + old_part, :]
    top = dot_left(lower_ref[0], rows_ref[0:NB, :]).astype(BF)
    for s in range(slots):
        block = cols_ref[pcol * slots + s]
        right[0:NB, lanes(s)] = jnp.where(block >= 1, -top[:, lanes(s)], jnp.zeros((NB, NB), BF))
    mid = (rows_ref[NB:TOP, :].astype(F32) + dot(low_ref[...], right[0:NB, :])).astype(BF)
    low = dot_left(lower_ref[1], mid).astype(BF)
    for s in range(slots):
        block = cols_ref[pcol * slots + s]
        right[NB:TOP, lanes(s)] = jnp.where(block >= 2, -low[:, lanes(s)], jnp.zeros((NB, NB), BF))

    dest = local_row(jnp.concatenate([index_vec[0:1, :], index_vec[1:2, :]], axis=1), prow, prow_count)
    copies = []
    for step in range(steps):
        lines = slice(step * block_rows, (step + 1) * block_rows)
        stage = stages.at[step % 2]
        if step >= 2:
            copies[step - 2].wait()
        loads[step].wait()
        line = lax.broadcasted_iota(jnp.int32, (block_rows, TOP), 0) + step * block_rows
        hot = jnp.where(line == dest, 1.0, 0.0)
        kept = jnp.sum(hot, axis=1, keepdims=True) == 0.0
        left = jnp.concatenate([l_ref[lines, :], hot.astype(BF)], axis=1)
        old = a_ref[lines, :].astype(F32)
        stage[...] = (jnp.where(kept, old, 0.0) + dot(left, right[...])).astype(BF)
        for k in range(2):
            slot = index_ref[TOP + k]

            @pl.when(slot // slots == pcol)
            def _():
                start = pl.multiple_of(slot % slots * NB, NB)
                stage[:, pl.ds(start, NB)] = l_ref[lines, k * NB:(k + 1) * NB]

        if step == 0:

            @pl.when(prow == 0)
            def _():
                for s in range(slots):
                    block = cols_ref[pcol * slots + s]
                    stage[0:NB, lanes(s)] = jnp.where(block >= 1, -right[0:NB, lanes(s)], rows_ref[0:NB, lanes(s)])

            @pl.when(prow == 1)
            def _():
                for s in range(slots):
                    block = cols_ref[pcol * slots + s]
                    changed = jnp.where(block == 1, mid[:, lanes(s)], -right[NB:TOP, lanes(s)])
                    stage[0:NB, lanes(s)] = jnp.where(block == 0, low_ref[...], changed)

        copies.append(pltpu.make_async_copy(stage, out_ref.at[pl.ds(step * block_rows, block_rows), :], sems.at[step % 2]))
        copies[step].start()
    for copy in copies[-2:]:
        copy.wait()


def update(where, index, col_blocks, parts, low, lower_inv, matrix, left, prow_count):
    rows_here, cols_here = matrix.shape
    smem = pl.BlockSpec(memory_space=pltpu.SMEM)
    vmem = pl.BlockSpec(memory_space=pltpu.VMEM)
    return pl.pallas_call(
        lambda *refs: update_kernel(prow_count, *refs),
        out_shape=jax.ShapeDtypeStruct(matrix.shape, BF),
        in_specs=[smem] * 3 + [vmem] * (1 + prow_count + 3) + [pl.BlockSpec(memory_space=pltpu.HBM)],
        out_specs=pl.BlockSpec(memory_space=pltpu.HBM),
        scratch_shapes=[
            pltpu.VMEM(matrix.shape, BF),
            pltpu.VMEM((TOP, cols_here), BF),
            pltpu.VMEM((2 * TOP, cols_here), BF),
            pltpu.VMEM((2, rows_here // STEPS, cols_here), BF),
            pltpu.SemaphoreType.DMA((2,)),
            pltpu.SemaphoreType.DMA((STEPS,)),
        ],
        compiler_params=pltpu.CompilerParams(vmem_limit_bytes=VMEM_BYTES),
        name="update",
    )(where, index, col_blocks, index.reshape(-1, NB), *parts, low, lower_inv, left, matrix)


CORE_SWAP = [(i, i ^ 1) for i in range(PY * PX * CORES)]
CHIP_GROUPS = [[i * CORES + c for i in range(PY * PX)] for c in range(CORES)]


def spread(x, axis, groups, count):
    x = jnp.broadcast_to(x[None], (count,) + x.shape)
    return lax.all_to_all(x, axis, 0, 0, axis_index_groups=groups)


def local(matrix, pivots, col_blocks, lower_inv, upper_inv):
    prow_count = lax.axis_size("prow")
    prow = lax.axis_index("prow")
    pcol = lax.axis_index("pcol")
    core = pcol % CORES
    where = jnp.stack([prow, pcol, core]).astype(jnp.int32)
    slots = matrix.shape[1] // NB

    meta = jnp.concatenate([pivots, col_blocks.reshape(-1, NB)], axis=0)
    index, parts, own, send = fetch(where, meta, matrix, prow_count)
    barrier = lax.optimization_barrier
    ups = [(i, (i + 1) % prow_count) for i in range(prow_count)]
    downs = [(i, (i - 1) % prow_count) for i in range(prow_count)]

    def part_at(offset):
        return lax.dynamic_index_in_dim(parts, (prow + offset) % prow_count, 0, keepdims=False)

    def go_up(x, step):
        x = lax.ppermute(x, "prow", ups)
        if step == 1:
            x, _ = barrier((x, panel))
        return x + part_at(4 - step)

    def go_down(x, step):
        x = lax.ppermute(x, "prow", downs)
        return x + part_at(step - 3) if step < 3 else x

    got = {}

    def gather_step(step):
        got[step] = lax.ppermute(got[step - 1], "prow", ups)
        if step < 4:
            got[prow_count - step] = lax.ppermute(got[(prow_count - step + 1) % prow_count], "prow", downs)

    state = {}

    def ring(names):
        for name in names.split():
            kind, step = name[0], int(name[1])
            if kind == "U":
                state["up"] = go_up(state["up"] if step > 1 else part_at(4), step)
            elif kind == "D":
                state["down"] = go_down(state["down"] if step > 1 else part_at(-3), step)
            elif kind == "G":
                if step == 1:
                    got[0] = state.pop("up") + state.pop("down")
                gather_step(step)

    def fence(panel, extra=()):
        flat, tree = jax.tree.flatten((panel, dict(got), dict(state), extra))
        panel, now, then, extra = jax.tree.unflatten(tree, barrier(flat))
        got.update(now)
        state.update(then)
        return panel, extra

    owner = lax.dynamic_index_in_dim(index[TOP:TOP + 2], core, 0, keepdims=False) // slots
    chip = owner // CORES
    chunk_top = SMALL // CHUNKS
    panel = own + lax.ppermute(send, "pcol", CORE_SWAP)
    ring(PLAN[0])
    panel = lax.all_to_all(panel, "pcol", 0, 0, axis_index_groups=CHIP_GROUPS)
    ring(PLAN[1])
    panel, chip = fence(panel, chip)

    panel = lax.dynamic_index_in_dim(panel, chip, 0, keepdims=False)
    small = jnp.sum(spread(panel[:chunk_top], "prow", None, prow_count), axis=0, dtype=BF)
    panel = jnp.concatenate([small, panel[chunk_top:]], axis=0)
    ring(PLAN[2])
    panel, _ = fence(panel)

    mine = spread(panel, "pcol", CHIP_GROUPS, CHUNKS)
    ring(PLAN[3])
    mine, _ = fence(mine)
    ring(PLAN[4])
    other = lax.ppermute(mine, "pcol", CORE_SWAP)

    left, low = factor(where, index, mine, other, lower_inv, upper_inv, prow_count)
    return update(where, index, col_blocks, [got[s] for s in range(prow_count)], low, lower_inv, matrix, left, prow_count)


def solution(mesh):
    in_specs = (P("prow", "pcol"), P(), P(), P(), P())
    out_specs = P("prow", "pcol")
    return jax.shard_map(local, mesh=mesh, in_specs=in_specs, out_specs=out_specs, check_vma=False)
```

```python
import jax
import jax.numpy as jnp
from jax import lax
from jax.experimental import pallas as pl
from jax.experimental.pallas import tpu as pltpu
from jax.sharding import PartitionSpec as P

NB = 128
TOP = 2 * NB
PY, PX, CORES = 4, 4, 2
CHUNKS = PY * PX
SMALL = 4 * NB
STEPS = 4
PLAN = ("D1 U1", "D2 U2 D3 U3", "U4 G1", "G2 G3", "G4")
VMEM_BYTES = 50 * 1024 * 1024

BF = jnp.bfloat16
F32 = jnp.float32


def split3(x):
    high = x.astype(BF)
    rest = x - high.astype(F32)
    mid = rest.astype(BF)
    low = (rest - mid.astype(F32)).astype(BF)
    return high, mid, low


def dot(a, b):
    return jnp.dot(a, b, preferred_element_type=F32)


def dot_right(x, w):
    high, mid, low = split3(w)
    return dot(x, low) + dot(x, mid) + dot(x, high)


def dot_left(w, x):
    high, mid, low = split3(w)
    return dot(low, x) + dot(mid, x) + dot(high, x)


def local_row(rows, prow, prow_count):
    here = (rows // NB) % prow_count == prow
    return jnp.where(here & (rows >= 0), rows // (NB * prow_count) * NB + rows % NB, -1)


def fetch_kernel(where_ref, meta_ref, a_ref, index_ref, parts_ref, own_ref, send_ref, order, piv_ref, held, slab, picked, old, sems, panel_sems, top_sems):
    prow, core = where_ref[0], where_ref[2]
    prow_count = parts_ref.shape[0]
    slots = a_ref.shape[1] // NB
    chunk_top = SMALL // CHUNKS
    block_rows = a_ref.shape[0] // CHUNKS
    top_part, old_part = TOP // prow_count, NB // prow_count
    piv_copy = pltpu.make_async_copy(meta_ref.at[pl.ds(0, 2), :], piv_ref, top_sems.at[0])
    old_copy = pltpu.make_async_copy(a_ref.at[pl.ds(0, NB), :], old, top_sems.at[1])
    piv_copy.start()
    old_copy.start()
    at = lax.broadcasted_iota(jnp.int32, (2, NB), 0) * NB + lax.broadcasted_iota(jnp.int32, (2, NB), 1)
    places = [
        jnp.sum(jnp.where(meta_ref[2:4, :] == k, at, 0).astype(F32)).astype(jnp.int32) for k in range(2)
    ]
    panels = []
    for n, (out, panel) in enumerate(((own_ref, core), (send_ref, 1 - core))):
        place = jnp.where(panel == 0, places[0], places[1])
        start = pl.multiple_of(place % slots * NB, NB)
        copies = [
            pltpu.make_async_copy(
                a_ref.at[pl.ds(j * block_rows, block_rows), pl.ds(start, NB)],
                out.at[j, pl.ds(chunk_top, block_rows), :],
                panel_sems.at[n, j],
            )
            for j in range(CHUNKS)
        ]
        panels.append((out, panel, start, place // slots % CORES == core, copies))

        @pl.when(panels[n][3])
        def _():
            for copy in copies:
                copy.start()

    for k in range(2):
        index_ref[TOP + k] = places[k]

    def init(t, carry):
        order[t] = t
        index_ref[t] = -1
        return carry

    lax.fori_loop(0, TOP, init, 0, unroll=TOP)
    piv_copy.wait()

    def untouched(t):
        far = piv_ref[t // NB, t % NB]
        order[far] = far

    for t in range(TOP):
        untouched(t)

    def exchange(t):
        far = piv_ref[t // NB, t % NB]
        near_value = order[t]
        far_value = order[far]
        order[t] = far_value
        order[far] = near_value

    for t in range(TOP):
        exchange(t)

    def collect(g, count):
        held[count] = g
        return count + ((order[g] >> 7) & (prow_count - 1) == prow).astype(jnp.int32)

    count = lax.fori_loop(0, TOP, collect, 0, unroll=TOP)

    def line_of(n):
        row = order[held[n]]
        return (row >> 10) * NB + (row & (NB - 1))

    def slab_copy(n, line):
        first = pl.multiple_of(line >> 4 << 4, 16)
        return pltpu.make_async_copy(a_ref.at[pl.ds(first, 16), :], slab.at[n], sems.at[n])

    def begin(n, carry):
        slab_copy(n, line_of(n)).start()
        return carry

    lax.fori_loop(0, count, begin, 0)
    picked[...] = jnp.zeros_like(picked)

    def emit(t):
        far = piv_ref[t // NB, t % NB]
        index_ref[jnp.where(far >= TOP, order[far], TOP + NB)] = far

    for t in range(TOP):
        emit(t)
    line16 = lax.broadcasted_iota(jnp.int32, (16, a_ref.shape[1]), 0)

    def take(n, carry):
        line = line_of(n)
        slab_copy(n, line).wait()
        chosen = jnp.where(line16 == (line & 15), slab[n].astype(F32), 0.0)
        picked[pl.ds(held[n], 1), :] = jnp.sum(chosen, axis=0, keepdims=True)
        return carry

    lax.fori_loop(0, count, take, 0)
    old_copy.wait()
    for q in range(prow_count):
        parts_ref[q, 0:top_part, :] = picked[q * top_part:(q + 1) * top_part, :].astype(BF)
        for k in range(2):
            first = top_part + k * old_part
            mine = old[q * old_part:(q + 1) * old_part, :]
            parts_ref[q, first:first + old_part, :] = jnp.where(prow == k, mine, jnp.zeros_like(mine))
    for out, panel, start, valid, copies in panels:

        @pl.when(valid)
        def _():
            near = picked[pl.ds(pl.multiple_of((1 - panel) * NB, NB), NB), pl.ds(start, NB)].astype(BF)
            far = old[:, pl.ds(start, NB)]
            zero = jnp.zeros_like(far)
            small = jnp.concatenate([near, jnp.where(prow == 0, far, zero), jnp.where(prow == 1, far, zero), zero], axis=0)
            for copy in copies:
                copy.wait()
            for j in range(CHUNKS):
                out[j, 0:chunk_top, :] = small[j * chunk_top:(j + 1) * chunk_top]

        @pl.when(jnp.logical_not(valid))
        def _():
            out[...] = jnp.zeros_like(out)


def fetch(where, meta, matrix, prow_count):
    rows_here, cols_here = matrix.shape
    chunk = (rows_here + SMALL) // CHUNKS
    part = 2 * TOP // prow_count
    smem = pl.BlockSpec(memory_space=pltpu.SMEM)
    vmem = pl.BlockSpec(memory_space=pltpu.VMEM)
    hbm = pl.BlockSpec(memory_space=pltpu.HBM)
    return pl.pallas_call(
        fetch_kernel,
        out_shape=(
            jax.ShapeDtypeStruct((2 * TOP,), jnp.int32),
            jax.ShapeDtypeStruct((prow_count, part, cols_here), BF),
            jax.ShapeDtypeStruct((CHUNKS, chunk, NB), BF),
            jax.ShapeDtypeStruct((CHUNKS, chunk, NB), BF),
        ),
        in_specs=[smem, vmem, hbm],
        out_specs=(smem, vmem, vmem, vmem),
        scratch_shapes=[
            pltpu.SMEM((rows_here * prow_count,), jnp.int32),
            pltpu.SMEM((2, NB), jnp.int32),
            pltpu.SMEM((TOP + 1,), jnp.int32),
            pltpu.VMEM((TOP, 16, cols_here), BF),
            pltpu.VMEM((TOP, cols_here), F32),
            pltpu.VMEM((NB, cols_here), BF),
            pltpu.SemaphoreType.DMA((TOP,)),
            pltpu.SemaphoreType.DMA((2, CHUNKS)),
            pltpu.SemaphoreType.DMA((2,)),
        ],
        compiler_params=pltpu.CompilerParams(vmem_limit_bytes=VMEM_BYTES),
        name="fetch",
    )(where, meta, matrix)


def factor_kernel(prow_count, where_ref, index_vec, mine_ref, other_ref, lower_ref, upper_ref, out_ref, low_ref):
    prow, core = where_ref[0], where_ref[2]
    chunk = mine_ref.shape[1]
    chunk_top = SMALL // CHUNKS
    block_rows = chunk - chunk_top

    def panel(k, j, part):
        mine, other = mine_ref[j, part, :], other_ref[j, part, :]
        return jnp.where(core == k, mine, other)

    small = [jnp.concatenate([panel(k, j, slice(0, chunk_top)) for j in range(CHUNKS)], axis=0) for k in range(2)]
    near_mid, near_top = small[0][0:NB], small[1][0:NB]
    far = [small[0][NB:NB + TOP], small[1][NB:NB + TOP]]
    top_mid = dot_left(lower_ref[0], near_top).astype(BF)
    low_ref[...] = dot_right(near_mid, upper_ref[0]).astype(BF)
    dest = local_row(jnp.concatenate([index_vec[0:1, :], index_vec[1:2, :]], axis=1), prow, prow_count)
    group = CHUNKS // PY
    block_rows *= group
    for j in range(PY):
        line = lax.broadcasted_iota(jnp.int32, (block_rows, TOP), 0) + j * block_rows
        hot = jnp.where(line == dest, 1.0, 0.0)
        kept = jnp.sum(hot, axis=1, keepdims=True) == 0.0
        hot = hot.astype(BF)
        raw = []
        for k in range(2):
            here = jnp.concatenate([panel(k, j * group + i, slice(chunk_top, chunk)) for i in range(group)], axis=0)
            raw.append(jnp.where(kept, here.astype(F32), dot(hot, far[k])))
        first = dot_right(raw[0].astype(BF), upper_ref[0]).astype(BF)
        if j == 0:
            above = (lax.broadcasted_iota(jnp.int32, (block_rows, NB), 0) < NB) & (prow == 0)
            first = jnp.where(above, jnp.zeros_like(first), first)
        middle = (raw[1] - dot(first, top_mid)).astype(BF)
        second = dot_right(middle, upper_ref[1]).astype(BF)
        if j == 0:
            above = (lax.broadcasted_iota(jnp.int32, (block_rows, NB), 0) < NB) & (prow < 2)
            second = jnp.where(above, jnp.zeros_like(second), second)
        out_ref[j * block_rows:(j + 1) * block_rows, 0:NB] = first
        out_ref[j * block_rows:(j + 1) * block_rows, NB:] = second


def factor(where, index, mine, other, lower_inv, upper_inv, prow_count):
    rows_here = CHUNKS * (mine.shape[1] - SMALL // CHUNKS)
    smem = pl.BlockSpec(memory_space=pltpu.SMEM)
    vmem = pl.BlockSpec(memory_space=pltpu.VMEM)
    return pl.pallas_call(
        lambda *refs: factor_kernel(prow_count, *refs),
        out_shape=(jax.ShapeDtypeStruct((rows_here, TOP), BF), jax.ShapeDtypeStruct((NB, NB), BF)),
        in_specs=[smem] + [vmem] * 5,
        out_specs=(vmem, vmem),
        compiler_params=pltpu.CompilerParams(vmem_limit_bytes=VMEM_BYTES),
        name="factor",
    )(where, index.reshape(-1, NB), mine, other, lower_inv, upper_inv)


def update_kernel(prow_count, where_ref, index_ref, cols_ref, index_vec, *refs):
    parts = refs[:prow_count]
    low_ref, lower_ref, l_ref, matrix_ref, out_ref, a_ref, rows_ref, right, stages, sems, load_sems = refs[prow_count:]
    prow, pcol = where_ref[0], where_ref[1]
    steps, block_rows = STEPS, a_ref.shape[0] // STEPS
    slots = a_ref.shape[1] // NB
    lanes = lambda s: slice(s * NB, (s + 1) * NB)
    loads = []
    for step in range(steps):
        lines = pl.ds(step * block_rows, block_rows)
        loads.append(pltpu.make_async_copy(matrix_ref.at[lines, :], a_ref.at[lines, :], load_sems.at[step]))
        loads[step].start()
    top_part, old_part = TOP // prow_count, NB // prow_count
    for shift, part in enumerate(parts):
        source = lax.rem(prow + prow_count - shift, prow_count)
        rows_ref[pl.ds(pl.multiple_of(source * top_part, top_part), top_part), :] = part[0:top_part, :]
        for k in range(2):
            first = top_part + k * old_part
            line = pl.multiple_of(TOP + k * NB + source * old_part, old_part)
            right[pl.ds(line, old_part), :] = part[first:first + old_part, :]
    top = dot_left(lower_ref[0], rows_ref[0:NB, :]).astype(BF)
    for s in range(slots):
        block = cols_ref[pcol * slots + s]
        right[0:NB, lanes(s)] = jnp.where(block >= 1, -top[:, lanes(s)], jnp.zeros((NB, NB), BF))
    mid = (rows_ref[NB:TOP, :].astype(F32) + dot(low_ref[...], right[0:NB, :])).astype(BF)
    low = dot_left(lower_ref[1], mid).astype(BF)
    for s in range(slots):
        block = cols_ref[pcol * slots + s]
        right[NB:TOP, lanes(s)] = jnp.where(block >= 2, -low[:, lanes(s)], jnp.zeros((NB, NB), BF))

    dest = local_row(jnp.concatenate([index_vec[0:1, :], index_vec[1:2, :]], axis=1), prow, prow_count)
    copies = []
    for step in range(steps):
        lines = slice(step * block_rows, (step + 1) * block_rows)
        stage = stages.at[step % 2]
        if step >= 2:
            copies[step - 2].wait()
        loads[step].wait()
        line = lax.broadcasted_iota(jnp.int32, (block_rows, TOP), 0) + step * block_rows
        hot = jnp.where(line == dest, 1.0, 0.0)
        kept = jnp.sum(hot, axis=1, keepdims=True) == 0.0
        left = jnp.concatenate([l_ref[lines, :], hot.astype(BF)], axis=1)
        old = a_ref[lines, :].astype(F32)
        stage[...] = (jnp.where(kept, old, 0.0) + dot(left, right[...])).astype(BF)
        for k in range(2):
            slot = index_ref[TOP + k]

            @pl.when(slot // slots == pcol)
            def _():
                start = pl.multiple_of(slot % slots * NB, NB)
                stage[:, pl.ds(start, NB)] = l_ref[lines, k * NB:(k + 1) * NB]

        if step == 0:

            @pl.when(prow == 0)
            def _():
                for s in range(slots):
                    block = cols_ref[pcol * slots + s]
                    stage[0:NB, lanes(s)] = jnp.where(block >= 1, -right[0:NB, lanes(s)], rows_ref[0:NB, lanes(s)])

            @pl.when(prow == 1)
            def _():
                for s in range(slots):
                    block = cols_ref[pcol * slots + s]
                    changed = jnp.where(block == 1, mid[:, lanes(s)], -right[NB:TOP, lanes(s)])
                    stage[0:NB, lanes(s)] = jnp.where(block == 0, low_ref[...], changed)

        copies.append(pltpu.make_async_copy(stage, out_ref.at[pl.ds(step * block_rows, block_rows), :], sems.at[step % 2]))
        copies[step].start()
    for copy in copies[-2:]:
        copy.wait()


def update(where, index, col_blocks, parts, low, lower_inv, matrix, left, prow_count):
    rows_here, cols_here = matrix.shape
    smem = pl.BlockSpec(memory_space=pltpu.SMEM)
    vmem = pl.BlockSpec(memory_space=pltpu.VMEM)
    return pl.pallas_call(
        lambda *refs: update_kernel(prow_count, *refs),
        out_shape=jax.ShapeDtypeStruct(matrix.shape, BF),
        in_specs=[smem] * 3 + [vmem] * (1 + prow_count + 3) + [pl.BlockSpec(memory_space=pltpu.HBM)],
        out_specs=pl.BlockSpec(memory_space=pltpu.HBM),
        scratch_shapes=[
            pltpu.VMEM(matrix.shape, BF),
            pltpu.VMEM((TOP, cols_here), BF),
            pltpu.VMEM((2 * TOP, cols_here), BF),
            pltpu.VMEM((2, rows_here // STEPS, cols_here), BF),
            pltpu.SemaphoreType.DMA((2,)),
            pltpu.SemaphoreType.DMA((STEPS,)),
        ],
        compiler_params=pltpu.CompilerParams(vmem_limit_bytes=VMEM_BYTES),
        name="update",
    )(where, index, col_blocks, index.reshape(-1, NB), *parts, low, lower_inv, left, matrix)


CORE_SWAP = [(i, i ^ 1) for i in range(PY * PX * CORES)]
CHIP_GROUPS = [[i * CORES + c for i in range(PY * PX)] for c in range(CORES)]


def spread(x, axis, groups, count):
    x = jnp.broadcast_to(x[None], (count,) + x.shape)
    return lax.all_to_all(x, axis, 0, 0, axis_index_groups=groups)


def local(matrix, pivots, col_blocks, lower_inv, upper_inv):
    prow_count = lax.axis_size("prow")
    prow = lax.axis_index("prow")
    pcol = lax.axis_index("pcol")
    core = pcol % CORES
    where = jnp.stack([prow, pcol, core]).astype(jnp.int32)
    slots = matrix.shape[1] // NB

    meta = jnp.concatenate([pivots, col_blocks.reshape(-1, NB)], axis=0)
    index, parts, own, send = fetch(where, meta, matrix, prow_count)
    barrier = lax.optimization_barrier
    ups = [(i, (i + 1) % prow_count) for i in range(prow_count)]
    downs = [(i, (i - 1) % prow_count) for i in range(prow_count)]

    def part_at(offset):
        return lax.dynamic_index_in_dim(parts, (prow + offset) % prow_count, 0, keepdims=False)

    def go_up(x, step):
        x = lax.ppermute(x, "prow", ups)
        if step == 1:
            x, _ = barrier((x, panel))
        return x + part_at(4 - step)

    def go_down(x, step):
        x = lax.ppermute(barrier((x, panel))[0] if step == 1 else x, "prow", downs)
        return x + part_at(step - 3) if step < 3 else x

    got = {}

    def gather_step(step):
        got[step] = lax.ppermute(got[step - 1], "prow", ups)
        if step < 4:
            got[prow_count - step] = lax.ppermute(got[(prow_count - step + 1) % prow_count], "prow", downs)

    state = {}

    def ring(names):
        for name in names.split():
            kind, step = name[0], int(name[1])
            if kind == "U":
                state["up"] = go_up(state["up"] if step > 1 else part_at(4), step)
            elif kind == "D":
                state["down"] = go_down(state["down"] if step > 1 else part_at(-3), step)
            elif kind == "G":
                if step == 1:
                    got[0] = state.pop("up") + state.pop("down")
                gather_step(step)

    def fence(panel, extra=()):
        flat, tree = jax.tree.flatten((panel, dict(got), dict(state), extra))
        panel, now, then, extra = jax.tree.unflatten(tree, barrier(flat))
        got.update(now)
        state.update(then)
        return panel, extra

    owner = lax.dynamic_index_in_dim(index[TOP:TOP + 2], core, 0, keepdims=False) // slots
    chip = owner // CORES
    chunk_top = SMALL // CHUNKS
    panel = own + lax.ppermute(send, "pcol", CORE_SWAP)
    ring(PLAN[0])
    panel = lax.all_to_all(panel, "pcol", 0, 0, axis_index_groups=CHIP_GROUPS)
    ring(PLAN[1])
    panel, chip = fence(panel, chip)

    panel = lax.dynamic_index_in_dim(panel, chip, 0, keepdims=False)
    small = jnp.sum(spread(panel[:chunk_top], "prow", None, prow_count), axis=0, dtype=BF)
    panel = jnp.concatenate([small, panel[chunk_top:]], axis=0)
    ring(PLAN[2])
    panel, _ = fence(panel)

    mine = spread(panel, "pcol", CHIP_GROUPS, CHUNKS)
    ring(PLAN[3])
    mine, _ = fence(mine)
    ring(PLAN[4])
    other = lax.ppermute(mine, "pcol", CORE_SWAP)

    left, low = factor(where, index, mine, other, lower_inv, upper_inv, prow_count)
    return update(where, index, col_blocks, [got[s] for s in range(prow_count)], low, lower_inv, matrix, left, prow_count)


def solution(mesh):
    in_specs = (P("prow", "pcol"), P(), P(), P(), P())
    out_specs = P("prow", "pcol")
    return jax.shard_map(local, mesh=mesh, in_specs=in_specs, out_specs=out_specs, check_vma=False)
```
